256 devices in a mesh: ctx: 16 (over x_lo, y, core), tp: 16 (over x_hi, z).
Axes of the slice: x: 4 (x_hi: 2, x_lo: 2; x = x_hi * 2 + x_lo), y: 4, z: 8, core: 2. Of those that a mesh axis runs over, the one named last changes fastest.
Arguments:
- queries: bfloat16 [2, 8192, 4096], P(None, 'ctx', 'tp'), may hold values from -5 to 5
- keys: bfloat16 [2, 8192, 512], P(None, 'ctx'), may hold values from -5 to 5
- values: bfloat16 [2, 8192, 512], P(None, 'ctx'), may hold values from -6 to 6
- output_matrix: bfloat16 [2, 4096, 8192], P(None, 'tp'), may hold values from -4 to 4
- adapter_down_weight: bfloat16 [2, 4096, 16], P(None, 'tp'), may hold values from -0.75 to 0.75
- adapter_up_weight: bfloat16 [16, 8192], P(None, 'tp'), may hold values from -6 to 6
Outputs:
- layer_out: bfloat16 [8192, 8192], P('ctx', 'tp')
The draws below stay inside these ranges and needn't reach their ends.
All inputs are finite; a program needn't handle non-finite values.
Results may differ from the reference program's by a relative error of at most 0.0054.
Values may be sent and summed in bfloat16 or wider, within the bound.
A program may use at most 128 MiB of HBM per device.

```python
import math
import jax
import jax.numpy as jnp
from jax import lax

MODEL_WIDTH = 8192
QUERY_HEADS = 64
KVH = 8
HEAD_SIZE = 128
ADAPTER_RANK = 16
TOKENS = 8192
GROUP = 2048
SHIFT = 1024


def draw_queries(key, part):
    key = jax.random.fold_in(key, 11)
    full_shape = (2, TOKENS, QUERY_HEADS // 2, HEAD_SIZE)
    sample = jnp.clip(jax.random.normal(key, full_shape, jnp.float32), -4.0, 4.0)
    return sample.reshape(2, TOKENS, QUERY_HEADS // 2 * HEAD_SIZE).astype(jnp.bfloat16)


def draw_keys(key, part):
    key = jax.random.fold_in(key, 23)
    full_shape = (2, TOKENS, KVH // 2, HEAD_SIZE)
    sample = jnp.clip(jax.random.normal(key, full_shape, jnp.float32), -4.0, 4.0)
    return sample.reshape(2, TOKENS, KVH // 2 * HEAD_SIZE).astype(jnp.bfloat16)


def with_spikes(entries, stream_key, source, target, shards_of, factor):
    def block_of(position):
        return (jnp.arange(entries.shape[position]) // (entries.shape[position] // shards_of)).reshape((-1,) + (1,) * (entries.ndim - 1 - position))

    near = jax.random.permutation(stream_key, shards_of)[block_of(target)]
    other_side = (block_of(target) + shards_of // 2) % shards_of
    return jnp.where((block_of(source) == near) | (block_of(source) == other_side), factor * entries, entries)


def shard_levels(rng, shape, shards, least, top_value):
    def one(position, parts):
        draws = jax.random.uniform(jax.random.fold_in(jax.random.fold_in(rng, 6), position), (parts,), jnp.float32, least / len(shards), top_value / len(shards))
        return jnp.repeat(jnp.exp(draws), shape[position] // parts).reshape((-1,) + (1,) * (len(shape) - position - 1))

    gain = one(*shards[0])
    for cut in shards[1:]:
        gain = gain * one(*cut)
    return gain


def centred(rng, dims, scale, reach, shards=(), kind=jnp.bfloat16):
    factor_of = shard_levels(rng, dims, shards, -0.22, 0.18) if shards else 1.0
    entries = jax.random.normal(rng, dims, jnp.float32) * scale * factor_of
    return jnp.minimum(jnp.maximum(entries, -reach), reach).astype(kind)


def gaussian_with(own_key, dims, spread, bound, cuts, heavy, kind=jnp.bfloat16):
    array = spread * jax.random.normal(own_key, dims, jnp.float32)
    if cuts:
        array = array * shard_levels(own_key, dims, cuts, -0.22, 0.18)
    return jnp.clip(with_spikes(array, jax.random.fold_in(own_key, 3), *heavy), -bound, bound).astype(kind)


def setup_inputs(seed: int = 0) -> dict:
    key_list = jax.random.split(jax.random.key(seed), 7)
    return {
        "queries": draw_queries(jax.random.fold_in(key_list[6], 71), 0),
        "keys": draw_keys(jax.random.fold_in(key_list[6], 71), 0),
        "values": centred(key_list[2], (2, TOKENS, KVH // 2 * HEAD_SIZE), 1.0, 6.0, ((1, 16),)),
        "output_matrix": gaussian_with(key_list[3], (2, QUERY_HEADS // 2 * HEAD_SIZE, MODEL_WIDTH), 0.2, 4.0, ((1, 16),), (1, 2, 16, 2.0)),
        "adapter_down_weight": centred(key_list[4], (2, QUERY_HEADS // 2 * HEAD_SIZE, ADAPTER_RANK), 0.05, 0.75, ((1, 16),)),
        "adapter_up_weight": centred(key_list[5], (ADAPTER_RANK, MODEL_WIDTH), 0.5, 6.0, ((1, 16),)),
    }


ADAPTER_SCALE = 2.0

def group_attention(triple):
    q_group, k_group, v_group = triple
    scores = jnp.einsum('rqd,kd->rqk', q_group.astype(jnp.float32), k_group.astype(jnp.float32)) * (1.0 / math.sqrt(HEAD_SIZE))
    allowed = jnp.tril(jnp.ones((GROUP, GROUP), dtype=bool))
    scores = jnp.where(allowed[None], scores, -jnp.inf)
    row_max = lax.optimization_barrier(jnp.max(scores, axis=-1, keepdims=True))
    expo = jnp.exp(scores - row_max)
    denom = lax.optimization_barrier(jnp.sum(expo, axis=-1, keepdims=True))
    weights = expo.astype(jnp.bfloat16)
    summed = jnp.einsum('rqk,kd->rqd', weights.astype(jnp.float32), v_group.astype(jnp.float32))
    return (summed / denom).astype(jnp.bfloat16)

def half_attention(queries, keys, values):
    repeats = QUERY_HEADS // KVH
    kv_half = KVH // 2
    groups = TOKENS // GROUP
    q_all = queries.reshape(groups, GROUP, kv_half, repeats, HEAD_SIZE).transpose(0, 2, 3, 1, 4).reshape(groups * kv_half, repeats, GROUP, HEAD_SIZE)
    k_all = keys.reshape(groups, GROUP, kv_half, HEAD_SIZE).transpose(0, 2, 1, 3).reshape(groups * kv_half, GROUP, HEAD_SIZE)
    v_all = values.reshape(groups, GROUP, kv_half, HEAD_SIZE).transpose(0, 2, 1, 3).reshape(groups * kv_half, GROUP, HEAD_SIZE)
    result = lax.map(group_attention, (q_all, k_all, v_all))
    return result.reshape(groups, kv_half, repeats, GROUP, HEAD_SIZE).transpose(0, 3, 1, 2, 4).reshape(TOKENS, QUERY_HEADS // 2 * HEAD_SIZE)

def reference(queries, keys, values, output_matrix, adapter_down_weight, adapter_up_weight):
    plain = half_attention(queries[0], keys[0], values[0])
    rolled = half_attention(jnp.roll(queries[1], -SHIFT, axis=0), jnp.roll(keys[1], -SHIFT, axis=0), jnp.roll(values[1], -SHIFT, axis=0))
    shifted = jnp.roll(rolled, SHIFT, axis=0)
    attention = jnp.stack([plain, shifted])
    merged_heads = attention.transpose(1, 0, 2).reshape(TOKENS, QUERY_HEADS * HEAD_SIZE)
    projected_output = jnp.dot(merged_heads, output_matrix.reshape(QUERY_HEADS * HEAD_SIZE, MODEL_WIDTH), preferred_element_type=jnp.float32)
    narrow_product = jnp.dot(merged_heads, adapter_down_weight.reshape(QUERY_HEADS * HEAD_SIZE, ADAPTER_RANK), preferred_element_type=jnp.float32)
    adapter_output = jnp.dot(narrow_product, adapter_up_weight.astype(jnp.float32), precision=lax.Precision.HIGHEST)
    return (projected_output + ADAPTER_SCALE * adapter_output).astype(jnp.bfloat16)
```

```python
import functools
import math

import jax
import jax.numpy as jnp
from jax import lax
from jax.experimental import pallas as pl
from jax.experimental.pallas import tpu as pltpu
from jax.sharding import PartitionSpec as P

HEAD = 128
ROWS = 512
LANES = 4
LANE = 128
RANK = 16
COLS = 512
HALF_COLS = 256
ADAPTER_SCALE = 2.0
SCORE_SCALE = math.log2(math.e) / math.sqrt(HEAD)
MESH = pl.DeviceIdType.MESH
F32 = jnp.float32
BF16 = jnp.bfloat16

ORDER = (4, 3, 5, 2, 6, 1, 7, 0)
GROUPS = ((0, 1), (1, 2), (3, 2), (5, 3))
STEP_CHUNK = ((0, 1, 3, 5, 7), (0, 2, 4, 6, 7))


def dot(a, b):
    return jnp.dot(a, b, preferred_element_type=F32)


def dot_nt(a, b):
    return lax.dot_general(a, b, (((1,), (1,)), ((), ())), preferred_element_type=F32)


def kernel(
    q_ref, k_hbm, v_hbm, w_hbm, down_ref, up_ref, out_ref,
    kvo, kvs, kvp, wn, wo, att_o, att_x, dt_o, dt_x, up_all, low3,
    m_ref, l_ref, acc_ref, c_ref, h0s, h0r, o1s, r1, r2, r3,
    loc_sem, wn_sem, kv_s, kv_r, up_s, up_r, ax_s, ax_r,
    wx_s, wx_r, wy_s, wy_r, ws_s, ws_r, rs_s, rs_r,
):
    ctx = lax.axis_index("ctx")
    tp = lax.axis_index("tp")
    core = ctx % 2
    y = (ctx // 2) % 4
    x_lo = ctx // 8
    z = tp % 8
    x_hi = tp // 8

    def at_z(k):
        return (ctx, x_hi * 8 + (z + k) % 8)

    def at_y(k):
        return ((x_lo * 4 + (y + k) % 4) * 2 + core, tp)

    sibling = (x_lo * 8 + y * 2 + 1 - core, tp)
    nxt = ((ctx + 2) % 16, tp)
    prv = ((ctx + 14) % 16, tp)
    partner = (ctx, (1 - x_hi) * 8 + z)
    w_partner = ((1 - x_lo) * 8 + y * 2 + core, (1 - x_hi) * 8 + z)

    sent = []

    def copy(src, dst, ss, rs, dev):
        return pltpu.make_async_remote_copy(
            src_ref=src, dst_ref=dst, send_sem=ss, recv_sem=rs, device_id=dev, device_id_type=MESH
        )

    def send(src, dst, ss, rs, dev):
        one = copy(src, dst, ss, rs, dev)
        one.start()
        sent.append(one)

    def arrived(dst, ss, rs):
        copy(dst, dst, ss, rs, sibling).wait_recv()

    kv_col = pl.ds(pl.multiple_of((tp // 4) * HEAD, HEAD), HEAD)
    load_k = pltpu.make_async_copy(k_hbm.at[:, :, kv_col], kvo.at[0], loc_sem.at[0])
    load_v = pltpu.make_async_copy(v_hbm.at[:, :, kv_col], kvo.at[1], loc_sem.at[1])
    load_k.start()
    load_v.start()

    def col_of(hi, i):
        return pl.ds(pl.multiple_of((hi * 8 + (z + ORDER[i]) % 8) * COLS, COLS), COLS)

    barrier = pltpu.get_barrier_semaphore()
    friends = [sibling, nxt, prv, partner, w_partner]
    friends += [at_y(k) for k in range(1, 4)] + [at_z(k) for k in range(1, 8)]
    for friend in friends:
        pl.semaphore_signal(barrier, inc=1, device_id=friend, device_id_type=MESH)

    ri = lax.broadcasted_iota(jnp.int32, (3 * RANK, RANK), 0)
    ci = lax.broadcasted_iota(jnp.int32, (3 * RANK, RANK), 1)
    eye3 = jnp.where((ri == ci) | (ri == ci + RANK) | (ri == ci + 2 * RANK), 1.0, 0.0).astype(BF16)
    for h in range(2):
        dt_o[h] = dot_nt(eye3, down_ref[h]).astype(BF16)
    up_all[z] = up_ref[...]

    pl.semaphore_wait(barrier, len(friends))

    small = y % 2
    large = 1 - small
    kv = (k_hbm, v_hbm)
    for j in range(2):
        send(kv[j].at[small, :, kv_col], kvp.at[j, core], kv_s.at[j], kv_r.at[j], nxt)
    to_sibling = [
        copy(kv[j].at[:, :, kv_col], kvs.at[j], kv_s.at[2 + j], kv_r.at[2 + j], sibling)
        for j in range(2)
    ]

    @pl.when(core == 0)
    def _():
        for one in to_sibling:
            one.start()

    w_half = y // 2

    def rows_of(who_y, who_core):
        return pl.ds(pl.multiple_of(((who_y % 2) * 2 + who_core) * 64, 64), 64)

    def import_chunk(i):
        send(
            w_hbm.at[w_half, rows_of(y, core), col_of(1 - x_hi, i)],
            wo.at[i, w_half, rows_of(y, core)],
            wx_s.at[i], wx_r.at[i], w_partner,
        )

    def forward(g):
        first, count = GROUPS[g]
        for i in range(first, first + count):
            arrived(wo.at[i, w_half, rows_of(y, core)], wx_s.at[i], wx_r.at[i])
        mine = wo.at[pl.ds(first, count), w_half, rows_of(y, core)]
        for k in range(1, 4):
            send(mine, mine, wy_s.at[g, k - 1], wy_r.at[g, k - 1], at_y(k))
        send(mine, mine, ws_s.at[g, 0], ws_r.at[g, 0], sibling)

    def pass_on(g):
        first, count = GROUPS[g]
        for k in range(1, 4):
            other = (y + 4 - k) % 4
            part = wo.at[pl.ds(first, count), other // 2, rows_of(other, core)]
            arrived(part, wy_s.at[g, k - 1], wy_r.at[g, k - 1])
            send(part, part, ws_s.at[g, k], ws_r.at[g, k], sibling)

    def ready(g):
        first, count = GROUPS[g]
        for k in range(4):
            other = (y + 4 - k) % 4
            part = wo.at[pl.ds(first, count), other // 2, rows_of(other, 1 - core)]
            arrived(part, ws_s.at[g, k], ws_r.at[g, k])

    for i in range(3):
        import_chunk(i)
    for k in range(1, 8):
        send(up_ref, up_all.at[z], up_s.at[k - 1], up_r.at[k - 1], at_z(k))
    send(dt_o, dt_x, ax_s.at[LANES], ax_r.at[LANES], partner)
    for i in range(3, 5):
        import_chunk(i)

    load_w = [
        pltpu.make_async_copy(w_hbm.at[:, :, col_of(x_hi, i)], wn.at[i], wn_sem.at[i]) for i in range(8)
    ]
    for one in load_w:
        one.start()

    load_k.wait()
    load_v.wait()

    def queries_of(h, lane):
        rows = pl.ds(pl.multiple_of(lane * LANE, LANE), LANE)
        return jnp.concatenate([q_ref[h, rows, 0:HEAD], q_ref[h, rows, HEAD:2 * HEAD]], axis=0)

    def own_keys(t, carry):
        h = (small + t) % 2
        for lane in range(LANES):
            q = queries_of(h, lane)
            edge = lane * LANE
            s1 = dot_nt(q, kvo[0, h, edge:edge + LANE, :]) * SCORE_SCALE
            row = lax.broadcasted_iota(jnp.int32, s1.shape, 0) % LANE
            col = lax.broadcasted_iota(jnp.int32, s1.shape, 1)
            s1 = jnp.where(col <= row, s1, -jnp.inf)
            m = jnp.max(s1, axis=1, keepdims=True)
            if lane:
                s0 = dot_nt(q, kvo[0, h, 0:edge, :]) * SCORE_SCALE
                m = jnp.maximum(m, jnp.max(s0, axis=1, keepdims=True))
            p1 = jnp.exp2(s1 - m)
            total = jnp.sum(p1, axis=1, keepdims=True)
            acc = dot(p1.astype(BF16), kvo[1, h, edge:edge + LANE, :])
            if lane:
                p0 = jnp.exp2(s0 - m)
                total = total + jnp.sum(p0, axis=1, keepdims=True)
                acc = acc + dot(p0.astype(BF16), kvo[1, h, 0:edge, :])
            m_ref[t, lane] = jnp.broadcast_to(m, (2 * LANE, HEAD))
            l_ref[t, lane] = jnp.broadcast_to(total, (2 * LANE, HEAD))
            acc_ref[t, lane] = acc
        return carry

    def more_keys(t, h, lane, keys, vals):
        s = dot_nt(queries_of(h, lane), keys) * SCORE_SCALE
        m_old = m_ref[t, lane][:, 0:1]
        m = jnp.maximum(m_old, jnp.max(s, axis=1, keepdims=True))
        scale = jnp.exp2(m_old - m)
        p = jnp.exp2(s - m)
        total = l_ref[t, lane][:, 0:1] * scale + jnp.sum(p, axis=1, keepdims=True)
        acc = acc_ref[t, lane] * scale + dot(p.astype(BF16), vals)
        return m, total, acc

    lax.fori_loop(0, 2, own_keys, 0)
    forward(0)
    forward(1)

    @pl.when(core == 1)
    def _():
        for j in range(2):
            to_sibling[j].wait_recv()

        def sibling_keys(n, carry):
            t = n // LANES
            lane = n % LANES
            h = (small + t) % 2
            m, total, acc = more_keys(t, h, lane, kvs[0, h], kvs[1, h])
            m_ref[t, lane] = jnp.broadcast_to(m, (2 * LANE, HEAD))
            l_ref[t, lane] = jnp.broadcast_to(total, (2 * LANE, HEAD))
            acc_ref[t, lane] = acc
            return carry

        lax.fori_loop(0, 2 * LANES, sibling_keys, 0)

    for j in range(2):
        arrived(kvp.at[j, core], kv_s.at[j], kv_r.at[j])
        send(kvp.at[j, core], kvp.at[j, core], kv_s.at[4 + j], kv_r.at[4 + j], sibling)
    for j in range(2):
        arrived(kvp.at[j, 1 - core], kv_s.at[4 + j], kv_r.at[4 + j])

    def finish(h, lane, total, acc):
        att = (acc / total).astype(BF16)
        att_o[lane, h, :, 0:HEAD] = att[0:LANE]
        att_o[lane, h, :, HEAD:2 * HEAD] = att[LANE:2 * LANE]

    for lane in range(LANES):
        finish(small, lane, l_ref[0, lane][:, 0:1], acc_ref[0, lane])
        keys = kvp[0].reshape(2 * ROWS, HEAD)
        vals = kvp[1].reshape(2 * ROWS, HEAD)
        _, total, acc = more_keys(1, large, lane, keys, vals)
        finish(large, lane, total, acc)
        send(att_o.at[lane], att_x.at[lane], ax_s.at[lane], ax_r.at[lane], partner)

    for i in range(5, 8):
        import_chunk(i)

    pass_on(0)
    arrived(dt_x, ax_s.at[LANES], ax_r.at[LANES])
    for k in range(1, 8):
        arrived(up_all.at[(z + 8 - k) % 8], up_s.at[k - 1], up_r.at[k - 1])
    for i in range(3):
        load_w[i].wait()
    ready(0)

    def product(i, half, own, other, low):
        cols = slice(half * HALF_COLS, (half + 1) * HALF_COLS)
        up = up_all[(z + ORDER[i]) % 8, :, cols]
        out = dot(low, jnp.concatenate([up, up, up], axis=0))
        for h in range(2):
            out = out + dot(own[h], wn[i, h, :, cols]) + dot(other[h], wo[i, h, :, cols])
        return out

    def operands(first, count):
        rows = slice(first, first + count)
        own = [att_o[rows, h].reshape(count * LANE, 2 * HEAD) for h in range(2)]
        other = [att_x[rows, h].reshape(count * LANE, 2 * HEAD) for h in range(2)]
        return own, other, low3[rows].reshape(count * LANE, 3 * RANK)

    ring = (at_z(1), at_z(7))
    for pair in range(2):
        for lane in range(2 * pair, 2 * pair + 2):
            arrived(att_x.at[lane], ax_s.at[lane], ax_r.at[lane])
            low = jnp.zeros((LANE, 3 * RANK), F32)
            for h in range(2):
                low = low + dot_nt(att_o[lane, h], dt_o[h]) + dot_nt(att_x[lane, h], dt_x[h])
            low = low * ADAPTER_SCALE
            top = low.astype(BF16).astype(F32)
            rest = low - top
            mid = rest.astype(BF16).astype(F32)
            third = lax.broadcasted_iota(jnp.int32, low.shape, 1) // RANK
            low3[lane] = jnp.where(third == 0, top, jnp.where(third == 1, mid, rest - mid)).astype(BF16)
            own, other, low = operands(lane, 1)
            for d in range(2):
                h0s[d, lane] = product(0, d, own, other, low).astype(BF16)
                send(h0s.at[d, lane], h0r.at[d, lane], rs_s.at[d, lane, 0], rs_r.at[d, lane, 0], ring[d])
        if pair == 0:
            pass_on(1)
            ready(1)
        own, other, low = operands(2 * pair, 2)
        rows = slice(2 * pair * LANE, (2 * pair + 2) * LANE)
        for d in range(2):
            i = STEP_CHUNK[d][1]
            start = product(i, 1 - d, own, other, low).astype(BF16)
            for n in range(2):
                lane = 2 * pair + n
                o1s[d, lane] = start[n * LANE:(n + 1) * LANE]
                send(o1s.at[d, lane], r1.at[d, lane, 1 - d], rs_s.at[d, lane, 2], rs_r.at[d, lane, 2], ring[d])
        for d in range(2):
            i = STEP_CHUNK[d][1]
            c_ref[i, d, rows] = product(i, d, own, other, low)

    def whole_chunk(i):
        own, other, low = operands(0, LANES)
        for half in range(2):
            c_ref[i, half] = product(i, half, own, other, low)

    forward(2)
    for lane in range(LANES):
        rows = slice(lane * LANE, (lane + 1) * LANE)
        for d in range(2):
            slot = h0r.at[d, lane]
            arrived(slot, rs_s.at[d, lane, 0], rs_r.at[d, lane, 0])
            h0r[d, lane] = (h0r[d, lane].astype(F32) + c_ref[STEP_CHUNK[d][1], d, rows]).astype(BF16)
            send(slot, r1.at[d, lane, d], rs_s.at[d, lane, 1], rs_r.at[d, lane, 1], ring[d])
        if lane == 1:
            pass_on(2)
    forward(3)
    ready(2)
    for i in range(3, 5):
        load_w[i].wait()
        whole_chunk(i)

    def add_chunk(buf, d, lane, i):
        for half in range(2):
            rows = slice(lane * LANE, (lane + 1) * LANE)
            buf[d, lane, half] = (buf[d, lane, half].astype(F32) + c_ref[i, half, rows]).astype(BF16)

    for lane in range(LANES):
        for d in range(2):
            for half in range(2):
                msg = 1 if half == d else 2
                arrived(r1.at[d, lane, half], rs_s.at[d, lane, msg], rs_r.at[d, lane, msg])
            add_chunk(r1, d, lane, STEP_CHUNK[d][2])
            send(r1.at[d, lane], r2.at[d, lane], rs_s.at[d, lane, 3], rs_r.at[d, lane, 3], ring[d])
        if lane == 1:
            pass_on(3)
    ready(3)
    for i in range(5, 8):
        load_w[i].wait()
        whole_chunk(i)
    for lane in range(LANES):
        for d in range(2):
            arrived(r2.at[d, lane], rs_s.at[d, lane, 3], rs_r.at[d, lane, 3])
            add_chunk(r2, d, lane, STEP_CHUNK[d][3])
            send(r2.at[d, lane], r3.at[d, lane], rs_s.at[d, lane, 4], rs_r.at[d, lane, 4], ring[d])
    for lane in range(LANES):
        rows = slice(lane * LANE, (lane + 1) * LANE)
        for d in range(2):
            arrived(r3.at[d, lane], rs_s.at[d, lane, 4], rs_r.at[d, lane, 4])
        for half in range(2):
            total = c_ref[7, half, rows] + r3[0, lane, half].astype(F32) + r3[1, lane, half].astype(F32)
            out_ref[rows, half * HALF_COLS:(half + 1) * HALF_COLS] = total.astype(BF16)

    for one in sent:
        one.wait_send()

    @pl.when(core == 0)
    def _():
        for one in to_sibling:
            one.wait_send()


def body(queries, keys, values, output_matrix, adapter_down_weight, adapter_up_weight):
    vmem = pl.BlockSpec(memory_space=pltpu.VMEM)
    hbm = pl.BlockSpec(memory_space=pl.ANY)
    dma = pltpu.SemaphoreType.DMA
    return pl.pallas_call(
        kernel,
        out_shape=jax.ShapeDtypeStruct((ROWS, COLS), BF16),
        in_specs=[vmem, hbm, hbm, hbm, vmem, vmem],
        out_specs=vmem,
        scratch_shapes=[
            pltpu.VMEM((2, 2, ROWS, HEAD), BF16),
            pltpu.VMEM((2, 2, ROWS, HEAD), BF16),
            pltpu.VMEM((2, 2, ROWS, HEAD), BF16),
            pltpu.VMEM((8, 2, 256, COLS), BF16),
            pltpu.VMEM((8, 2, 256, COLS), BF16),
            pltpu.VMEM((LANES, 2, LANE, 256), BF16),
            pltpu.VMEM((LANES, 2, LANE, 256), BF16),
            pltpu.VMEM((2, 3 * RANK, 256), BF16),
            pltpu.VMEM((2, 3 * RANK, 256), BF16),
            pltpu.VMEM((8, RANK, COLS), BF16),
            pltpu.VMEM((LANES, LANE, 3 * RANK), BF16),
            pltpu.VMEM((2, LANES, 2 * LANE, HEAD), F32),
            pltpu.VMEM((2, LANES, 2 * LANE, HEAD), F32),
            pltpu.VMEM((2, LANES, 2 * LANE, HEAD), F32),
            pltpu.VMEM((8, 2, ROWS, HALF_COLS), F32),
            pltpu.VMEM((2, LANES, LANE, HALF_COLS), BF16),
            pltpu.VMEM((2, LANES, LANE, HALF_COLS), BF16),
            pltpu.VMEM((2, LANES, LANE, HALF_COLS), BF16),
            pltpu.VMEM((2, LANES, 2, LANE, HALF_COLS), BF16),
            pltpu.VMEM((2, LANES, 2, LANE, HALF_COLS), BF16),
            pltpu.VMEM((2, LANES, 2, LANE, HALF_COLS), BF16),
            dma((2,)), dma((8,)),
            dma((6,)), dma((6,)),
            dma((7,)), dma((7,)),
            dma((LANES + 1,)), dma((LANES + 1,)),
            dma((8,)), dma((8,)),
            dma((4, 3)), dma((4, 3)),
            dma((4, 4)), dma((4, 4)),
            dma((2, LANES, 5)), dma((2, LANES, 5)),
        ],
        compiler_params=pltpu.CompilerParams(
            collective_id=0, has_side_effects=True, vmem_limit_bytes=56 * 2**20
        ),
        cost_estimate=pl.CostEstimate(flops=6 * 10**9, bytes_accessed=12 * 2**20, transcendentals=3 * 10**6),
        name="attend_and_project",
    )(queries, keys, values, output_matrix, adapter_down_weight, adapter_up_weight)


def solution(mesh):
    return jax.shard_map(
        body,
        mesh=mesh,
        in_specs=(
            P(None, "ctx", "tp"),
            P(None, "ctx", None),
            P(None, "ctx", None),
            P(None, "tp", None),
            P(None, "tp", None),
            P(None, "tp"),
        ),
        out_specs=P("ctx", "tp"),
        check_vma=False,
    )
```

```python
import functools
import math

import jax
import jax.numpy as jnp
from jax import lax
from jax.experimental import pallas as pl
from jax.experimental.pallas import tpu as pltpu
from jax.sharding import PartitionSpec as P

HEAD = 128
ROWS = 512
LANES = 4
LANE = 128
RANK = 16
COLS = 512
HALF_COLS = 256
ADAPTER_SCALE = 2.0
SCORE_SCALE = math.log2(math.e) / math.sqrt(HEAD)
MESH = pl.DeviceIdType.MESH
F32 = jnp.float32
BF16 = jnp.bfloat16

ORDER = (4, 3, 5, 2, 6, 1, 7, 0)
GROUPS = ((0, 1), (1, 2), (3, 2), (5, 3))
STEP_CHUNK = ((0, 1, 3, 5, 7), (0, 2, 4, 6, 7))


def dot(a, b):
    return jnp.dot(a, b, preferred_element_type=F32)


def dot_nt(a, b):
    return lax.dot_general(a, b, (((1,), (1,)), ((), ())), preferred_element_type=F32)


def kernel(
    q_ref, k_hbm, v_hbm, w_hbm, down_ref, up_ref, out_ref,
    kvo, kvs, kvp, wn, wo, att_o, att_x, dt_o, dt_x, up_all, low3,
    m_ref, l_ref, acc_ref, c_ref, h0s, h0r, o1s, r1, r2, r3,
    loc_sem, wn_sem, kv_s, kv_r, up_s, up_r, ax_s, ax_r,
    wx_s, wx_r, wy_s, wy_r, ws_s, ws_r, rs_s, rs_r,
):
    ctx = lax.axis_index("ctx")
    tp = lax.axis_index("tp")
    core = ctx % 2
    y = (ctx // 2) % 4
    x_lo = ctx // 8
    z = tp % 8
    x_hi = tp // 8

    def at_z(k):
        return (ctx, x_hi * 8 + (z + k) % 8)

    def at_y(k):
        return ((x_lo * 4 + (y + k) % 4) * 2 + core, tp)

    sibling = (x_lo * 8 + y * 2 + 1 - core, tp)
    nxt = ((ctx + 2) % 16, tp)
    prv = ((ctx + 14) % 16, tp)
    partner = (ctx, (1 - x_hi) * 8 + z)
    w_partner = ((1 - x_lo) * 8 + y * 2 + core, (1 - x_hi) * 8 + z)

    def copy(src, dst, ss, rs, dev):
        return pltpu.make_async_remote_copy(
            src_ref=src, dst_ref=dst, send_sem=ss, recv_sem=rs, device_id=dev, device_id_type=MESH
        )

    def send(src, dst, ss, rs, dev):
        copy(src, dst, ss, rs, dev).start()

    def arrived(dst, rs):
        copy(dst, dst, kv_s.at[0], rs, sibling).wait_recv()

    def left(src, ss):
        copy(src, src, ss, kv_r.at[0], sibling).wait_send()

    kv_col = pl.ds(pl.multiple_of((tp // 4) * HEAD, HEAD), HEAD)
    load_k = pltpu.make_async_copy(k_hbm.at[:, :, kv_col], kvo.at[0], loc_sem.at[0])
    load_v = pltpu.make_async_copy(v_hbm.at[:, :, kv_col], kvo.at[1], loc_sem.at[1])
    load_k.start()
    load_v.start()

    def col_of(hi, i):
        return pl.ds(pl.multiple_of((hi * 8 + (z + ORDER[i]) % 8) * COLS, COLS), COLS)

    barrier = pltpu.get_barrier_semaphore()
    friends = [sibling, nxt, prv, partner, w_partner]
    friends += [at_y(k) for k in range(1, 4)] + [at_z(1), at_z(7)]
    for friend in friends:
        pl.semaphore_signal(barrier, inc=1, device_id=friend, device_id_type=MESH)

    for h in range(2):
        dt_o[h] = jnp.concatenate([down_ref[h]] * 3, axis=0)
    up_all[z] = up_ref[...]

    pl.semaphore_wait(barrier, len(friends))

    small = y % 2
    large = 1 - small
    kv = (k_hbm, v_hbm)
    for j in range(2):
        send(kv[j].at[small, :, kv_col], kvp.at[j, core], kv_s.at[j], kv_r.at[j], nxt)
    to_sibling = [
        copy(kv[j].at[:, :, kv_col], kvs.at[j], kv_s.at[2 + j], kv_r.at[2 + j], sibling)
        for j in range(2)
    ]

    @pl.when(core == 0)
    def _():
        for one in to_sibling:
            one.start()

    w_half = y // 2

    def rows_of(who_y, who_core):
        return pl.ds(pl.multiple_of(((who_y % 2) * 2 + who_core) * 64, 64), 64)

    def import_group(g):
        first, count = GROUPS[g]
        for i in range(first, first + count):
            send(
                w_hbm.at[w_half, rows_of(y, core), col_of(1 - x_hi, i)],
                wo.at[i, w_half, rows_of(y, core)],
                wx_s.at[0], wx_r.at[g], w_partner,
            )

    def group(g, half, rows):
        first, count = GROUPS[g]
        return wo.at[pl.ds(first, count), half, rows]

    def forward(g):
        mine = group(g, w_half, rows_of(y, core))
        arrived(mine, wx_r.at[g])
        for k in range(1, 4):
            send(mine, mine, wy_s.at[k - 1], wy_r.at[g, k - 1], at_y(k))
        send(mine, mine, ws_s.at[0], ws_r.at[g, 0], sibling)

    def pass_on(g):
        for k in range(1, 4):
            other = (y + 4 - k) % 4
            part = group(g, other // 2, rows_of(other, core))
            arrived(part, wy_r.at[g, k - 1])
            send(part, part, ws_s.at[k], ws_r.at[g, k], sibling)

    def ready(g):
        for k in range(4):
            other = (y + 4 - k) % 4
            arrived(group(g, other // 2, rows_of(other, 1 - core)), ws_r.at[g, k])

    def up_step(k):
        for d in range(2):
            if k == 4 and d == 1:
                continue
            slot = up_all.at[(z + (9 - k if d == 0 else k - 1)) % 8]
            if k > 1:
                arrived(slot, up_r.at[d, k - 2])
            send(slot, slot, up_s.at[0], up_r.at[d, k - 1], ring[d])

    ring = (at_z(1), at_z(7))
    up_step(1)
    for g in range(3):
        import_group(g)
    send(dt_o, dt_x, ax_s.at[0], ax_r.at[LANES], partner)

    load_w = [
        pltpu.make_async_copy(w_hbm.at[:, :, col_of(x_hi, i)], wn.at[i], wn_sem.at[i // 3]) for i in range(8)
    ]
    for one in load_w:
        one.start()

    def loaded(n):
        part = wn.at[3 * n:min(3 * n + 3, 8)]
        pltpu.make_async_copy(part, part, wn_sem.at[n]).wait()

    load_k.wait()
    load_v.wait()

    def queries_of(h, lane):
        rows = pl.ds(pl.multiple_of(lane * LANE, LANE), LANE)
        return jnp.concatenate([q_ref[h, rows, 0:HEAD], q_ref[h, rows, HEAD:2 * HEAD]], axis=0)

    def own_keys(t):
        h = (small + t) % 2
        for lane in range(LANES):
            q = queries_of(h, lane)
            edge = lane * LANE
            s1 = dot_nt(q, kvo[0, h, edge:edge + LANE, :]) * SCORE_SCALE
            row = lax.broadcasted_iota(jnp.int32, s1.shape, 0) % LANE
            col = lax.broadcasted_iota(jnp.int32, s1.shape, 1)
            s1 = jnp.where(col <= row, s1, -jnp.inf)
            m = jnp.max(s1, axis=1, keepdims=True)
            if lane:
                s0 = dot_nt(q, kvo[0, h, 0:edge, :]) * SCORE_SCALE
                m = jnp.maximum(m, jnp.max(s0, axis=1, keepdims=True))
            p1 = jnp.exp2(s1 - m)
            total = jnp.sum(p1, axis=1, keepdims=True)
            acc = dot(p1.astype(BF16), kvo[1, h, edge:edge + LANE, :])
            if lane:
                p0 = jnp.exp2(s0 - m)
                total = total + jnp.sum(p0, axis=1, keepdims=True)
                acc = acc + dot(p0.astype(BF16), kvo[1, h, 0:edge, :])
            m_ref[t, lane] = jnp.broadcast_to(m, (2 * LANE, HEAD))
            l_ref[t, lane] = jnp.broadcast_to(total, (2 * LANE, HEAD))
            acc_ref[t, lane] = acc

    def more_keys(t, h, lane, keys, vals):
        s = dot_nt(queries_of(h, lane), keys) * SCORE_SCALE
        m_old = m_ref[t, lane][:, 0:1]
        m = jnp.maximum(m_old, jnp.max(s, axis=1, keepdims=True))
        scale = jnp.exp2(m_old - m)
        p = jnp.exp2(s - m)
        total = l_ref[t, lane][:, 0:1] * scale + jnp.sum(p, axis=1, keepdims=True)
        acc = acc_ref[t, lane] * scale + dot(p.astype(BF16), vals)
        return m, total, acc

    def keep(t, lane, state):
        m, total, acc = state
        m_ref[t, lane] = jnp.broadcast_to(m, (2 * LANE, HEAD))
        l_ref[t, lane] = jnp.broadcast_to(total, (2 * LANE, HEAD))
        acc_ref[t, lane] = acc

    def finish(h, lane, total, acc):
        att = (acc / total).astype(BF16)
        att_o[h, lane, :, 0:HEAD] = att[0:LANE]
        att_o[h, lane, :, HEAD:2 * HEAD] = att[LANE:2 * LANE]

    def sibling_keys(t):
        h = (small + t) % 2

        def one_lane(lane, carry):
            keep(t, lane, more_keys(t, h, lane, kvs[0, h], kvs[1, h]))
            return carry

        lax.fori_loop(0, LANES, one_lane, 0)

    own_keys(0)

    @pl.when(core == 1)
    def _():
        for j in range(2):
            to_sibling[j].wait_recv()
        sibling_keys(0)

    for lane in range(LANES):
        finish(small, lane, l_ref[0, lane][:, 0:1], acc_ref[0, lane])
    send(att_o.at[small], att_x.at[small], ax_s.at[0], ax_r.at[LANES + 1], partner)
    forward(0)
    up_step(2)
    own_keys(1)

    @pl.when(core == 1)
    def _():
        sibling_keys(1)

    up_step(3)
    for j in range(2):
        arrived(kvp.at[j, core], kv_r.at[j])
        send(kvp.at[j, core], kvp.at[j, core], kv_s.at[4], kv_r.at[4 + j], sibling)

    forward(1)

    def pair_keys(lane, carry):
        keep(1, lane, more_keys(1, large, lane, kvp[0, core], kvp[1, core]))
        return carry

    lax.fori_loop(0, LANES, pair_keys, 0)
    pass_on(0)
    for j in range(2):
        arrived(kvp.at[j, 1 - core], kv_r.at[4 + j])
    for lane in range(LANES):
        _, total, acc = more_keys(1, large, lane, kvp[0, 1 - core], kvp[1, 1 - core])
        finish(large, lane, total, acc)
        send(att_o.at[large, lane], att_x.at[large, lane], ax_s.at[0], ax_r.at[lane], partner)
    import_group(3)
    forward(2)

    up_step(4)
    arrived(dt_x, ax_r.at[LANES])
    arrived(att_x.at[small], ax_r.at[LANES + 1])
    arrived(up_all.at[(z + 4) % 8], up_r.at[0, 3])
    arrived(up_all.at[(z + 3) % 8], up_r.at[1, 2])
    loaded(0)
    ready(0)

    def product(i, half, own, other, low):
        cols = slice(half * HALF_COLS, (half + 1) * HALF_COLS)
        up = up_all[(z + ORDER[i]) % 8, :, cols]
        out = dot(low, jnp.concatenate([up, up, up], axis=0))
        for h in range(2):
            out = out + dot(own[h], wn[i, h, :, cols]) + dot(other[h], wo[i, h, :, cols])
        return out

    def operands(first, count):
        rows = slice(first, first + count)
        own = [att_o[h, rows].reshape(count * LANE, 2 * HEAD) for h in range(2)]
        other = [att_x[h, rows].reshape(count * LANE, 2 * HEAD) for h in range(2)]
        return own, other, low3[rows].reshape(count * LANE, 3 * RANK)

    for lane in range(LANES):
        arrived(att_x.at[large, lane], ax_r.at[lane])
        low = jnp.zeros((LANE, 3 * RANK), F32)
        for h in range(2):
            low = low + dot_nt(att_o[h, lane], dt_o[h]) + dot_nt(att_x[h, lane], dt_x[h])
        low = low * ADAPTER_SCALE
        top = low.astype(BF16).astype(F32)
        rest = low - top
        mid = rest.astype(BF16).astype(F32)
        third = lax.broadcasted_iota(jnp.int32, low.shape, 1) // RANK
        low3[lane] = jnp.where(third == 0, top, jnp.where(third == 1, mid, rest - mid)).astype(BF16)
        own, other, low = operands(lane, 1)
        for d in range(2):
            h0s[d, lane] = product(0, d, own, other, low).astype(BF16)
            send(h0s.at[d, lane], h0r.at[d, lane], rs_s.at[0], rs_r.at[d, lane, 0], ring[d])
        if lane == 0:
            pass_on(1)
    ready(1)
    own, other, low = operands(0, LANES)
    for d in range(2):
        start = product(STEP_CHUNK[d][1], 1 - d, own, other, low).astype(BF16)
        for lane in range(LANES):
            o1s[d, lane] = start[lane * LANE:(lane + 1) * LANE]
            send(o1s.at[d, lane], r1.at[d, lane, 1 - d], rs_s.at[2], rs_r.at[d, lane, 2], ring[d])
    for d in range(2):
        i = STEP_CHUNK[d][1]
        c_ref[i, d] = product(i, d, own, other, low)
    pass_on(2)
    forward(3)

    def whole_chunk(i):
        own, other, low = operands(0, LANES)
        for half in range(2):
            c_ref[i, half] = product(i, half, own, other, low)

    for lane in range(LANES):
        rows = slice(lane * LANE, (lane + 1) * LANE)
        for d in range(2):
            slot = h0r.at[d, lane]
            arrived(slot, rs_r.at[d, lane, 0])
            h0r[d, lane] = (h0r[d, lane].astype(F32) + c_ref[STEP_CHUNK[d][1], d, rows]).astype(BF16)
            send(slot, r1.at[d, lane, d], rs_s.at[1], rs_r.at[d, lane, 1], ring[d])
    ready(2)
    loaded(1)
    for i in range(3, 5):
        whole_chunk(i)

    def add_chunk(buf, d, lane, i):
        for half in range(2):
            rows = slice(lane * LANE, (lane + 1) * LANE)
            buf[d, lane, half] = (buf[d, lane, half].astype(F32) + c_ref[i, half, rows]).astype(BF16)

    for lane in range(LANES):
        for d in range(2):
            for half in range(2):
                msg = 1 if half == d else 2
                arrived(r1.at[d, lane, half], rs_r.at[d, lane, msg])
            add_chunk(r1, d, lane, STEP_CHUNK[d][2])
            send(r1.at[d, lane], r2.at[d, lane], rs_s.at[3], rs_r.at[d, lane, 3], ring[d])
    pass_on(3)
    loaded(2)
    ready(3)
    for i in range(5, 7):
        whole_chunk(i)
    for lane in range(LANES):
        for d in range(2):
            arrived(r2.at[d, lane], rs_r.at[d, lane, 3])
            add_chunk(r2, d, lane, STEP_CHUNK[d][3])
            send(r2.at[d, lane], r3.at[d, lane], rs_s.at[4], rs_r.at[d, lane, 4], ring[d])
    whole_chunk(7)
    for lane in range(LANES):
        rows = slice(lane * LANE, (lane + 1) * LANE)
        for d in range(2):
            arrived(r3.at[d, lane], rs_r.at[d, lane, 4])
        for half in range(2):
            total = c_ref[7, half, rows] + r3[0, lane, half].astype(F32) + r3[1, lane, half].astype(F32)
            out_ref[rows, half * HALF_COLS:(half + 1) * HALF_COLS] = total.astype(BF16)

    for n, buf in enumerate((h0s, h0r, o1s, r1, r2)):
        left(buf, rs_s.at[n])
    part = wo.at[:, 0, 0:64]
    left(part, wx_s.at[0])
    for k in range(1, 4):
        left(part, wy_s.at[k - 1])
    for k in range(4):
        left(part, ws_s.at[k])
    left(up_all.at[0:7], up_s.at[0])
    left(att_o, ax_s.at[0])
    left(dt_o, ax_s.at[0])
    for j in range(2):
        left(kvp.at[j, 0], kv_s.at[j])
    left(kvp.at[:, 0], kv_s.at[4])

    @pl.when(core == 0)
    def _():
        for one in to_sibling:
            one.wait_send()


def body(queries, keys, values, output_matrix, adapter_down_weight, adapter_up_weight):
    vmem = pl.BlockSpec(memory_space=pltpu.VMEM)
    hbm = pl.BlockSpec(memory_space=pl.ANY)
    dma = pltpu.SemaphoreType.DMA
    return pl.pallas_call(
        kernel,
        out_shape=jax.ShapeDtypeStruct((ROWS, COLS), BF16),
        in_specs=[vmem, hbm, hbm, hbm, vmem, vmem],
        out_specs=vmem,
        scratch_shapes=[
            pltpu.VMEM((2, 2, ROWS, HEAD), BF16),
            pltpu.VMEM((2, 2, ROWS, HEAD), BF16),
            pltpu.VMEM((2, 2, ROWS, HEAD), BF16),
            pltpu.VMEM((8, 2, 256, COLS), BF16),
            pltpu.VMEM((8, 2, 256, COLS), BF16),
            pltpu.VMEM((2, LANES, LANE, 256), BF16),
            pltpu.VMEM((2, LANES, LANE, 256), BF16),
            pltpu.VMEM((2, 3 * RANK, 256), BF16),
            pltpu.VMEM((2, 3 * RANK, 256), BF16),
            pltpu.VMEM((8, RANK, COLS), BF16),
            pltpu.VMEM((LANES, LANE, 3 * RANK), BF16),
            pltpu.VMEM((2, LANES, 2 * LANE, HEAD), F32),
            pltpu.VMEM((2, LANES, 2 * LANE, HEAD), F32),
            pltpu.VMEM((2, LANES, 2 * LANE, HEAD), F32),
            pltpu.VMEM((8, 2, ROWS, HALF_COLS), F32),
            pltpu.VMEM((2, LANES, LANE, HALF_COLS), BF16),
            pltpu.VMEM((2, LANES, LANE, HALF_COLS), BF16),
            pltpu.VMEM((2, LANES, LANE, HALF_COLS), BF16),
            pltpu.VMEM((2, LANES, 2, LANE, HALF_COLS), BF16),
            pltpu.VMEM((2, LANES, 2, LANE, HALF_COLS), BF16),
            pltpu.VMEM((2, LANES, 2, LANE, HALF_COLS), BF16),
            dma((2,)), dma((3,)),
            dma((5,)), dma((6,)),
            dma((1,)), dma((2, 4)),
            dma((1,)), dma((LANES + 2,)),
            dma((1,)), dma((4,)),
            dma((3,)), dma((4, 3)),
            dma((4,)), dma((4, 4)),
            dma((5,)), dma((2, LANES, 5)),
        ],
        compiler_params=pltpu.CompilerParams(
            collective_id=0, has_side_effects=True, vmem_limit_bytes=56 * 2**20
        ),
        cost_estimate=pl.CostEstimate(flops=6 * 10**9, bytes_accessed=12 * 2**20, transcendentals=3 * 10**6),
        name="attend_and_project",
    )(queries, keys, values, output_matrix, jnp.swapaxes(adapter_down_weight, 1, 2), adapter_up_weight)


def solution(mesh):
    return jax.shard_map(
        body,
        mesh=mesh,
        in_specs=(
            P(None, "ctx", "tp"),
            P(None, "ctx", None),
            P(None, "ctx", None),
            P(None, "tp", None),
            P(None, "tp", None),
            P(None, "tp"),
        ),
        out_specs=P("ctx", "tp"),
        check_vma=False,
    )
```

```python
import functools
import math

import jax
import jax.numpy as jnp
from jax import lax
from jax.experimental import pallas as pl
from jax.experimental.pallas import tpu as pltpu
from jax.sharding import PartitionSpec as P

HEAD = 128
ROWS = 512
LANES = 4
LANE = 128
RANK = 16
COLS = 512
HALF_COLS = 256
ADAPTER_SCALE = 2.0
SCORE_SCALE = math.log2(math.e) / math.sqrt(HEAD)
MESH = pl.DeviceIdType.MESH
F32 = jnp.float32
BF16 = jnp.bfloat16

ORDER = (4, 3, 5, 2, 6, 1, 7, 0)
PIECES = ((0, 0), (0, 1), (1, 1), (2, 0), (1, 0), (2, 1)) + tuple((i, half) for i in range(3, 8) for half in range(2))
GROUPS = ((0, 2), (2, 2), (4, 2), (6, 4), (10, 6))
STEP_CHUNK = ((0, 1, 3, 5, 7), (0, 2, 4, 6, 7))


def dot(a, b):
    return jnp.dot(a, b, preferred_element_type=F32)


def dot_nt(a, b):
    return lax.dot_general(a, b, (((1,), (1,)), ((), ())), preferred_element_type=F32)


def kernel(
    q_ref, k_hbm, v_hbm, w_hbm, down_ref, up_ref, out_ref,
    kvo, kvs, kvp, wn, wo, att_o, att_x, dt_o, dt_x, up_all, low3,
    m_ref, l_ref, acc_ref, c_ref, h0s, h0r, o1s, r1, r2, r3,
    loc_sem, wn_sem, kv_s, kv_r, up_s, up_r, ax_s, ax_r,
    wx_s, wx_r, wy_s, wy_r, ws_s, ws_r, rs_s, rs_r,
):
    ctx = lax.axis_index("ctx")
    tp = lax.axis_index("tp")
    core = ctx % 2
    y = (ctx // 2) % 4
    x_lo = ctx // 8
    z = tp % 8
    x_hi = tp // 8

    def at_z(k):
        return (ctx, x_hi * 8 + (z + k) % 8)

    def at_y(k):
        return ((x_lo * 4 + (y + k) % 4) * 2 + core, tp)

    sibling = (x_lo * 8 + y * 2 + 1 - core, tp)
    nxt = ((ctx + 2) % 16, tp)
    prv = ((ctx + 14) % 16, tp)
    partner = (ctx, (1 - x_hi) * 8 + z)
    w_partner = ((1 - x_lo) * 8 + y * 2 + core, (1 - x_hi) * 8 + z)

    def copy(src, dst, ss, rs, dev):
        return pltpu.make_async_remote_copy(
            src_ref=src, dst_ref=dst, send_sem=ss, recv_sem=rs, device_id=dev, device_id_type=MESH
        )

    def send(src, dst, ss, rs, dev):
        copy(src, dst, ss, rs, dev).start()

    def arrived(dst, rs):
        copy(dst, dst, kv_s.at[0], rs, sibling).wait_recv()

    def left(src, ss):
        copy(src, src, ss, kv_r.at[0], sibling).wait_send()

    kv_col = pl.ds(pl.multiple_of((tp // 4) * HEAD, HEAD), HEAD)
    load_k = pltpu.make_async_copy(k_hbm.at[:, :, kv_col], kvo.at[0], loc_sem.at[0])
    load_v = pltpu.make_async_copy(v_hbm.at[:, :, kv_col], kvo.at[1], loc_sem.at[1])
    load_k.start()
    load_v.start()

    def col_of(hi, i, half=0, width=COLS):
        first = (hi * 8 + (z + ORDER[i]) % 8) * COLS + half * HALF_COLS
        return pl.ds(pl.multiple_of(first, width), width)

    barrier = pltpu.get_barrier_semaphore()
    friends = [sibling, nxt, prv, partner, w_partner]
    friends += [at_y(k) for k in range(1, 4)] + [at_z(1), at_z(7)]
    for friend in friends:
        pl.semaphore_signal(barrier, inc=1, device_id=friend, device_id_type=MESH)

    for h in range(2):
        dt_o[h] = jnp.concatenate([down_ref[h]] * 3, axis=0)
    up_all[z] = up_ref[...]

    pl.semaphore_wait(barrier, len(friends))

    w_half = y // 2

    def rows_of(who_y, who_core):
        return pl.ds(pl.multiple_of(((who_y % 2) * 2 + who_core) * 64, 64), 64)

    def import_group(g):
        first, count = GROUPS[g]
        for n in range(first, first + count):
            send(
                w_hbm.at[w_half, rows_of(y, core), col_of(1 - x_hi, *PIECES[n], HALF_COLS)],
                wo.at[n, w_half, rows_of(y, core)],
                wx_s.at[0], wx_r.at[g], w_partner,
            )

    def group(g, half, rows):
        first, count = GROUPS[g]
        return wo.at[pl.ds(first, count), half, rows]

    def landed(g):
        arrived(group(g, w_half, rows_of(y, core)), wx_r.at[g])

    def forward(g):
        mine = group(g, w_half, rows_of(y, core))
        for k in range(1, 4):
            send(mine, mine, wy_s.at[k - 1], wy_r.at[g, k - 1], at_y(k))
        send(mine, mine, ws_s.at[0], ws_r.at[g, 0], sibling)

    def pass_on(g):
        for k in range(1, 4):
            other = (y + 4 - k) % 4
            part = group(g, other // 2, rows_of(other, core))
            arrived(part, wy_r.at[g, k - 1])
            send(part, part, ws_s.at[k], ws_r.at[g, k], sibling)

    def ready(g):
        for k in range(4):
            other = (y + 4 - k) % 4
            arrived(group(g, other // 2, rows_of(other, 1 - core)), ws_r.at[g, k])

    def up_step(k):
        for d in range(2):
            if k == 4 and d == 1:
                continue
            slot = up_all.at[(z + (9 - k if d == 0 else k - 1)) % 8]
            if k > 1:
                arrived(slot, up_r.at[d, k - 2])
            send(slot, slot, up_s.at[0], up_r.at[d, k - 1], ring[d])

    ring = (at_z(1), at_z(7))
    for g in range(3):
        import_group(g)

    small = y % 2
    large = 1 - small
    kv = (k_hbm, v_hbm)
    for j in range(2):
        send(kv[j].at[small, :, kv_col], kvp.at[j, core], kv_s.at[j], kv_r.at[j], nxt)
    to_sibling = [
        copy(kv[j].at[:, :, kv_col], kvs.at[j], kv_s.at[2 + j], kv_r.at[2 + j], sibling)
        for j in range(2)
    ]

    @pl.when(core == 0)
    def _():
        for one in to_sibling:
            one.start()

    send(dt_o, dt_x, ax_s.at[0], ax_r.at[LANES], partner)

    up_step(1)

    load_w = [
        pltpu.make_async_copy(w_hbm.at[:, :, col_of(x_hi, i)], wn.at[i], wn_sem.at[i // 3]) for i in range(8)
    ]
    for one in load_w:
        one.start()

    def loaded(n):
        part = wn.at[3 * n:min(3 * n + 3, 8)]
        pltpu.make_async_copy(part, part, wn_sem.at[n]).wait()

    load_k.wait()
    load_v.wait()

    def queries_of(h, lane):
        rows = pl.ds(pl.multiple_of(lane * LANE, LANE), LANE)
        return jnp.concatenate([q_ref[h, rows, 0:HEAD], q_ref[h, rows, HEAD:2 * HEAD]], axis=0)

    def own_keys(t):
        h = (small + t) % 2
        for lane in range(LANES):
            q = queries_of(h, lane)
            edge = lane * LANE
            s1 = dot_nt(q, kvo[0, h, edge:edge + LANE, :]) * SCORE_SCALE
            row = lax.broadcasted_iota(jnp.int32, s1.shape, 0) % LANE
            col = lax.broadcasted_iota(jnp.int32, s1.shape, 1)
            s1 = jnp.where(col <= row, s1, -jnp.inf)
            m = jnp.max(s1, axis=1, keepdims=True)
            if lane:
                s0 = dot_nt(q, kvo[0, h, 0:edge, :]) * SCORE_SCALE
                m = jnp.maximum(m, jnp.max(s0, axis=1, keepdims=True))
            p1 = jnp.exp2(s1 - m)
            total = jnp.sum(p1, axis=1, keepdims=True)
            acc = dot(p1.astype(BF16), kvo[1, h, edge:edge + LANE, :])
            if lane:
                p0 = jnp.exp2(s0 - m)
                total = total + jnp.sum(p0, axis=1, keepdims=True)
                acc = acc + dot(p0.astype(BF16), kvo[1, h, 0:edge, :])
            m_ref[t, lane] = jnp.broadcast_to(m, (2 * LANE, HEAD))
            l_ref[t, lane] = jnp.broadcast_to(total, (2 * LANE, HEAD))
            acc_ref[t, lane] = acc

    def more_keys(t, h, lane, keys, vals):
        s = dot_nt(queries_of(h, lane), keys) * SCORE_SCALE
        m_old = m_ref[t, lane][:, 0:1]
        m = jnp.maximum(m_old, jnp.max(s, axis=1, keepdims=True))
        scale = jnp.exp2(m_old - m)
        p = jnp.exp2(s - m)
        total = l_ref[t, lane][:, 0:1] * scale + jnp.sum(p, axis=1, keepdims=True)
        acc = acc_ref[t, lane] * scale + dot(p.astype(BF16), vals)
        return m, total, acc

    def keep(t, lane, state):
        m, total, acc = state
        m_ref[t, lane] = jnp.broadcast_to(m, (2 * LANE, HEAD))
        l_ref[t, lane] = jnp.broadcast_to(total, (2 * LANE, HEAD))
        acc_ref[t, lane] = acc

    def finish(h, lane, total, acc):
        att = (acc / total).astype(BF16)
        att_o[h, lane, :, 0:HEAD] = att[0:LANE]
        att_o[h, lane, :, HEAD:2 * HEAD] = att[LANE:2 * LANE]

    def sibling_keys(t):
        h = (small + t) % 2

        def one_lane(lane, carry):
            keep(t, lane, more_keys(t, h, lane, kvs[0, h], kvs[1, h]))
            return carry

        lax.fori_loop(0, LANES, one_lane, 0)

    own_keys(0)

    @pl.when(core == 1)
    def _():
        for j in range(2):
            to_sibling[j].wait_recv()
        sibling_keys(0)

    for lane in range(LANES):
        finish(small, lane, l_ref[0, lane][:, 0:1], acc_ref[0, lane])
    for g in range(3):
        landed(g)
    forward(0)
    send(att_o.at[small], att_x.at[small], ax_s.at[0], ax_r.at[LANES + 1], partner)
    import_group(3)
    up_step(2)
    own_keys(1)

    @pl.when(core == 1)
    def _():
        sibling_keys(1)

    up_step(3)
    for j in range(2):
        arrived(kvp.at[j, core], kv_r.at[j])
        send(kvp.at[j, core], kvp.at[j, core], kv_s.at[4], kv_r.at[4 + j], sibling)

    forward(1)
    forward(2)

    def pair_keys(lane, carry):
        keep(1, lane, more_keys(1, large, lane, kvp[0, core], kvp[1, core]))
        return carry

    lax.fori_loop(0, LANES, pair_keys, 0)
    up_step(4)
    pass_on(0)
    for j in range(2):
        arrived(kvp.at[j, 1 - core], kv_r.at[4 + j])
    for lane in range(LANES):
        _, total, acc = more_keys(1, large, lane, kvp[0, 1 - core], kvp[1, 1 - core])
        finish(large, lane, total, acc)
        send(att_o.at[large, lane], att_x.at[large, lane], ax_s.at[0], ax_r.at[lane], partner)
    import_group(4)
    pass_on(1)

    arrived(dt_x, ax_r.at[LANES])
    arrived(att_x.at[small], ax_r.at[LANES + 1])
    arrived(up_all.at[(z + 4) % 8], up_r.at[0, 3])
    arrived(up_all.at[(z + 3) % 8], up_r.at[1, 2])
    loaded(0)
    ready(0)

    def product(i, half, own, other, low):
        cols = slice(half * HALF_COLS, (half + 1) * HALF_COLS)
        n = PIECES.index((i, half))
        up = up_all[(z + ORDER[i]) % 8, :, cols]
        out = dot(low, jnp.concatenate([up, up, up], axis=0))
        for h in range(2):
            out = out + dot(own[h], wn[i, h, :, cols]) + dot(other[h], wo[n, h])
        return out

    def operands(first, count):
        rows = slice(first, first + count)
        own = [att_o[h, rows].reshape(count * LANE, 2 * HEAD) for h in range(2)]
        other = [att_x[h, rows].reshape(count * LANE, 2 * HEAD) for h in range(2)]
        return own, other, low3[rows].reshape(count * LANE, 3 * RANK)

    for lane in range(LANES):
        arrived(att_x.at[large, lane], ax_r.at[lane])
        low = jnp.zeros((LANE, 3 * RANK), F32)
        for h in range(2):
            low = low + dot_nt(att_o[h, lane], dt_o[h]) + dot_nt(att_x[h, lane], dt_x[h])
        low = low * ADAPTER_SCALE
        top = low.astype(BF16).astype(F32)
        rest = low - top
        mid = rest.astype(BF16).astype(F32)
        third = lax.broadcasted_iota(jnp.int32, low.shape, 1) // RANK
        low3[lane] = jnp.where(third == 0, top, jnp.where(third == 1, mid, rest - mid)).astype(BF16)
        own, other, low = operands(lane, 1)
        for d in range(2):
            h0s[d, lane] = product(0, d, own, other, low).astype(BF16)
            send(h0s.at[d, lane], h0r.at[d, lane], rs_s.at[0], rs_r.at[d, lane, 0], ring[d])
        if lane == 0:
            landed(3)
            forward(3)
        if lane == 1:
            pass_on(2)
    ready(1)
    own, other, low = operands(0, LANES)
    for d in range(2):
        start = product(STEP_CHUNK[d][1], 1 - d, own, other, low).astype(BF16)
        for lane in range(LANES):
            o1s[d, lane] = start[lane * LANE:(lane + 1) * LANE]
            send(o1s.at[d, lane], r1.at[d, lane, 1 - d], rs_s.at[2], rs_r.at[d, lane, 2], ring[d])
    ready(2)
    for d in range(2):
        i = STEP_CHUNK[d][1]
        c_ref[i, d] = product(i, d, own, other, low)
    pass_on(3)
    landed(4)
    forward(4)

    def whole_chunk(i):
        own, other, low = operands(0, LANES)
        for half in range(2):
            c_ref[i, half] = product(i, half, own, other, low)

    for lane in range(LANES):
        rows = slice(lane * LANE, (lane + 1) * LANE)
        for d in range(2):
            slot = h0r.at[d, lane]
            arrived(slot, rs_r.at[d, lane, 0])
            h0r[d, lane] = (h0r[d, lane].astype(F32) + c_ref[STEP_CHUNK[d][1], d, rows]).astype(BF16)
            send(slot, r1.at[d, lane, d], rs_s.at[1], rs_r.at[d, lane, 1], ring[d])
    loaded(1)
    ready(3)
    for i in range(3, 5):
        whole_chunk(i)

    def add_chunk(buf, d, lane, i):
        for half in range(2):
            rows = slice(lane * LANE, (lane + 1) * LANE)
            buf[d, lane, half] = (buf[d, lane, half].astype(F32) + c_ref[i, half, rows]).astype(BF16)

    for lane in range(LANES):
        for d in range(2):
            for half in range(2):
                msg = 1 if half == d else 2
                arrived(r1.at[d, lane, half], rs_r.at[d, lane, msg])
            add_chunk(r1, d, lane, STEP_CHUNK[d][2])
            send(r1.at[d, lane], r2.at[d, lane], rs_s.at[3], rs_r.at[d, lane, 3], ring[d])
    pass_on(4)
    loaded(2)
    ready(4)
    for i in range(5, 7):
        whole_chunk(i)
    for lane in range(LANES):
        for d in range(2):
            arrived(r2.at[d, lane], rs_r.at[d, lane, 3])
            add_chunk(r2, d, lane, STEP_CHUNK[d][3])
            send(r2.at[d, lane], r3.at[d, lane], rs_s.at[4], rs_r.at[d, lane, 4], ring[d])
    whole_chunk(7)
    for lane in range(LANES):
        rows = slice(lane * LANE, (lane + 1) * LANE)
        for d in range(2):
            arrived(r3.at[d, lane], rs_r.at[d, lane, 4])
        for half in range(2):
            total = c_ref[7, half, rows] + r3[0, lane, half].astype(F32) + r3[1, lane, half].astype(F32)
            out_ref[rows, half * HALF_COLS:(half + 1) * HALF_COLS] = total.astype(BF16)

    for n, buf in enumerate((h0s, h0r, o1s, r1, r2)):
        left(buf, rs_s.at[n])
    part = wo.at[:, 0, 0:64]
    left(part, wx_s.at[0])
    for k in range(1, 4):
        left(part, wy_s.at[k - 1])
    for k in range(4):
        left(part, ws_s.at[k])
    left(up_all.at[0:7], up_s.at[0])
    left(att_o, ax_s.at[0])
    left(dt_o, ax_s.at[0])
    for j in range(2):
        left(kvp.at[j, 0], kv_s.at[j])
    left(kvp.at[:, 0], kv_s.at[4])

    @pl.when(core == 0)
    def _():
        for one in to_sibling:
            one.wait_send()


def body(queries, keys, values, output_matrix, adapter_down_weight, adapter_up_weight):
    vmem = pl.BlockSpec(memory_space=pltpu.VMEM)
    hbm = pl.BlockSpec(memory_space=pl.ANY)
    dma = pltpu.SemaphoreType.DMA
    return pl.pallas_call(
        kernel,
        out_shape=jax.ShapeDtypeStruct((ROWS, COLS), BF16),
        in_specs=[vmem, hbm, hbm, hbm, vmem, vmem],
        out_specs=vmem,
        scratch_shapes=[
            pltpu.VMEM((2, 2, ROWS, HEAD), BF16),
            pltpu.VMEM((2, 2, ROWS, HEAD), BF16),
            pltpu.VMEM((2, 2, ROWS, HEAD), BF16),
            pltpu.VMEM((8, 2, 256, COLS), BF16),
            pltpu.VMEM((16, 2, 256, HALF_COLS), BF16),
            pltpu.VMEM((2, LANES, LANE, 256), BF16),
            pltpu.VMEM((2, LANES, LANE, 256), BF16),
            pltpu.VMEM((2, 3 * RANK, 256), BF16),
            pltpu.VMEM((2, 3 * RANK, 256), BF16),
            pltpu.VMEM((8, RANK, COLS), BF16),
            pltpu.VMEM((LANES, LANE, 3 * RANK), BF16),
            pltpu.VMEM((2, LANES, 2 * LANE, HEAD), F32),
            pltpu.VMEM((2, LANES, 2 * LANE, HEAD), F32),
            pltpu.VMEM((2, LANES, 2 * LANE, HEAD), F32),
            pltpu.VMEM((8, 2, ROWS, HALF_COLS), F32),
            pltpu.VMEM((2, LANES, LANE, HALF_COLS), BF16),
            pltpu.VMEM((2, LANES, LANE, HALF_COLS), BF16),
            pltpu.VMEM((2, LANES, LANE, HALF_COLS), BF16),
            pltpu.VMEM((2, LANES, 2, LANE, HALF_COLS), BF16),
            pltpu.VMEM((2, LANES, 2, LANE, HALF_COLS), BF16),
            pltpu.VMEM((2, LANES, 2, LANE, HALF_COLS), BF16),
            dma((2,)), dma((3,)),
            dma((5,)), dma((6,)),
            dma((1,)), dma((2, 4)),
            dma((1,)), dma((LANES + 2,)),
            dma((1,)), dma((5,)),
            dma((3,)), dma((5, 3)),
            dma((4,)), dma((5, 4)),
            dma((5,)), dma((2, LANES, 5)),
        ],
        compiler_params=pltpu.CompilerParams(
            collective_id=0, has_side_effects=True, vmem_limit_bytes=56 * 2**20
        ),
        cost_estimate=pl.CostEstimate(flops=6 * 10**9, bytes_accessed=12 * 2**20, transcendentals=3 * 10**6),
        name="attend_and_project",
    )(queries, keys, values, output_matrix, jnp.swapaxes(adapter_down_weight, 1, 2), adapter_up_weight)


def solution(mesh):
    return jax.shard_map(
        body,
        mesh=mesh,
        in_specs=(
            P(None, "ctx", "tp"),
            P(None, "ctx", None),
            P(None, "ctx", None),
            P(None, "tp", None),
            P(None, "tp", None),
            P(None, "tp"),
        ),
        out_specs=P("ctx", "tp"),
        check_vma=False,
    )
```

```python
import functools
import math

import jax
import jax.numpy as jnp
from jax import lax
from jax.experimental import pallas as pl
from jax.experimental.pallas import tpu as pltpu
from jax.sharding import PartitionSpec as P

HEAD = 128
ROWS = 512
LANES = 4
LANE = 128
RANK = 16
COLS = 512
HALF_COLS = 256
ADAPTER_SCALE = 2.0
SCORE_SCALE = math.log2(math.e) / math.sqrt(HEAD)
MESH = pl.DeviceIdType.MESH
F32 = jnp.float32
BF16 = jnp.bfloat16

ORDER = (4, 3, 5, 2, 6, 1, 7, 0)
PIECES = ((0, 0), (0, 1), (1, 1), (2, 0), (1, 0), (2, 1)) + tuple((i, half) for i in range(3, 8) for half in range(2))
GROUPS = ((0, 2), (2, 2), (4, 2), (6, 4), (10, 6))
STEP_CHUNK = ((0, 1, 3, 5, 7), (0, 2, 4, 6, 7))


def dot(a, b):
    return jnp.dot(a, b, preferred_element_type=F32)


def dot_nt(a, b):
    return lax.dot_general(a, b, (((1,), (1,)), ((), ())), preferred_element_type=F32)


def kernel(
    q_ref, k_hbm, v_hbm, w_hbm, down_ref, up_ref, out_ref,
    kvo, kvs, kvp, wn, wo, att_o, att_x, dt_o, dt_x, up_all, low3,
    m_ref, l_ref, acc_ref, c_ref, h0s, h0r, o1s, r1, r2, r3,
    loc_sem, wn_sem, kv_s, kv_r, up_s, up_r, ax_s, ax_r,
    wx_s, wx_r, wy_s, wy_r, ws_s, ws_r, rs_s, rs_r,
):
    ctx = lax.axis_index("ctx")
    tp = lax.axis_index("tp")
    core = ctx % 2
    y = (ctx // 2) % 4
    x_lo = ctx // 8
    z = tp % 8
    x_hi = tp // 8

    def at_z(k):
        return (ctx, x_hi * 8 + (z + k) % 8)

    def at_y(k):
        return ((x_lo * 4 + (y + k) % 4) * 2 + core, tp)

    sibling = (x_lo * 8 + y * 2 + 1 - core, tp)
    nxt = ((ctx + 2) % 16, tp)
    prv = ((ctx + 14) % 16, tp)
    partner = (ctx, (1 - x_hi) * 8 + z)
    w_partner = ((1 - x_lo) * 8 + y * 2 + core, (1 - x_hi) * 8 + z)

    def copy(src, dst, ss, rs, dev):
        return pltpu.make_async_remote_copy(
            src_ref=src, dst_ref=dst, send_sem=ss, recv_sem=rs, device_id=dev, device_id_type=MESH
        )

    def send(src, dst, ss, rs, dev):
        copy(src, dst, ss, rs, dev).start()

    def arrived(dst, rs):
        copy(dst, dst, kv_s.at[0], rs, sibling).wait_recv()

    def left(src, ss):
        copy(src, src, ss, kv_r.at[0], sibling).wait_send()

    kv_col = pl.ds(pl.multiple_of((tp // 4) * HEAD, HEAD), HEAD)
    load_k = pltpu.make_async_copy(k_hbm.at[:, :, kv_col], kvo.at[0], loc_sem.at[0])
    load_v = pltpu.make_async_copy(v_hbm.at[:, :, kv_col], kvo.at[1], loc_sem.at[1])
    load_k.start()
    load_v.start()

    def col_of(hi, i, half=0, width=COLS):
        first = (hi * 8 + (z + ORDER[i]) % 8) * COLS + half * HALF_COLS
        return pl.ds(pl.multiple_of(first, width), width)

    barrier = pltpu.get_barrier_semaphore()
    friends = [sibling, nxt, prv, partner, w_partner]
    friends += [at_y(k) for k in range(1, 4)] + [at_z(1), at_z(7)]
    for friend in friends:
        pl.semaphore_signal(barrier, inc=1, device_id=friend, device_id_type=MESH)

    for h in range(2):
        dt_o[h] = jnp.concatenate([down_ref[h]] * 3, axis=0)
    up_all[z] = up_ref[...]

    pl.semaphore_wait(barrier, len(friends))

    w_half = y // 2

    def rows_of(who_y, who_core):
        return pl.ds(pl.multiple_of(((who_y % 2) * 2 + who_core) * 64, 64), 64)

    def import_group(g):
        first, count = GROUPS[g]
        for n in range(first, first + count):
            send(
                w_hbm.at[w_half, rows_of(y, core), col_of(1 - x_hi, *PIECES[n], HALF_COLS)],
                wo.at[n, w_half, rows_of(y, core)],
                wx_s.at[0], wx_r.at[g], w_partner,
            )

    def group(g, half, rows):
        first, count = GROUPS[g]
        return wo.at[pl.ds(first, count), half, rows]

    def landed(g):
        arrived(group(g, w_half, rows_of(y, core)), wx_r.at[g])

    def forward(g):
        mine = group(g, w_half, rows_of(y, core))
        for k in range(1, 4):
            send(mine, mine, wy_s.at[k - 1], wy_r.at[g, k - 1], at_y(k))
        send(mine, mine, ws_s.at[0], ws_r.at[g, 0], sibling)

    def pass_on(g):
        for k in range(1, 4):
            other = (y + 4 - k) % 4
            part = group(g, other // 2, rows_of(other, core))
            arrived(part, wy_r.at[g, k - 1])
            send(part, part, ws_s.at[k], ws_r.at[g, k], sibling)

    def ready(g):
        for k in range(4):
            other = (y + 4 - k) % 4
            arrived(group(g, other // 2, rows_of(other, 1 - core)), ws_r.at[g, k])

    def up_step(k):
        for d in range(2):
            if k == 4 and d == 1:
                continue
            slot = up_all.at[(z + (9 - k if d == 0 else k - 1)) % 8]
            if k > 1:
                arrived(slot, up_r.at[d, k - 2])
            send(slot, slot, up_s.at[0], up_r.at[d, k - 1], ring[d])

    ring = (at_z(1), at_z(7))
    for g in range(3):
        import_group(g)

    small = y % 2
    large = 1 - small
    kv = (k_hbm, v_hbm)
    for j in range(2):
        send(kv[j].at[small, :, kv_col], kvp.at[j, core], kv_s.at[j], kv_r.at[j], nxt)
    to_sibling = [
        copy(kv[j].at[:, :, kv_col], kvs.at[j], kv_s.at[2 + j], kv_r.at[2 + j], sibling)
        for j in range(2)
    ]

    @pl.when(core == 0)
    def _():
        for one in to_sibling:
            one.start()

    send(dt_o, dt_x, ax_s.at[0], ax_r.at[LANES], partner)

    up_step(1)

    load_w = [
        pltpu.make_async_copy(w_hbm.at[:, :, col_of(x_hi, i)], wn.at[i], wn_sem.at[i // 3]) for i in range(8)
    ]
    for one in load_w:
        one.start()

    def loaded(n):
        part = wn.at[3 * n:min(3 * n + 3, 8)]
        pltpu.make_async_copy(part, part, wn_sem.at[n]).wait()

    load_k.wait()
    load_v.wait()

    def queries_of(h, lane):
        rows = pl.ds(pl.multiple_of(lane * LANE, LANE), LANE)
        return jnp.concatenate([q_ref[h, rows, 0:HEAD], q_ref[h, rows, HEAD:2 * HEAD]], axis=0)

    def own_keys(t):
        h = (small + t) % 2
        for lane in range(LANES):
            q = queries_of(h, lane)
            edge = lane * LANE
            s1 = dot_nt(q, kvo[0, h, edge:edge + LANE, :]) * SCORE_SCALE
            row = lax.broadcasted_iota(jnp.int32, s1.shape, 0) % LANE
            col = lax.broadcasted_iota(jnp.int32, s1.shape, 1)
            s1 = jnp.where(col <= row, s1, -jnp.inf)
            m = jnp.max(s1, axis=1, keepdims=True)
            if lane:
                s0 = dot_nt(q, kvo[0, h, 0:edge, :]) * SCORE_SCALE
                m = jnp.maximum(m, jnp.max(s0, axis=1, keepdims=True))
            p1 = jnp.exp2(s1 - m)
            total = jnp.sum(p1, axis=1, keepdims=True)
            acc = dot(p1.astype(BF16), kvo[1, h, edge:edge + LANE, :])
            if lane:
                p0 = jnp.exp2(s0 - m)
                total = total + jnp.sum(p0, axis=1, keepdims=True)
                acc = acc + dot(p0.astype(BF16), kvo[1, h, 0:edge, :])
            m_ref[t, lane] = jnp.broadcast_to(m, (2 * LANE, HEAD))
            l_ref[t, lane] = jnp.broadcast_to(total, (2 * LANE, HEAD))
            acc_ref[t, lane] = acc

    def more_keys(t, h, lane, keys, vals):
        s = dot_nt(queries_of(h, lane), keys) * SCORE_SCALE
        m_old = m_ref[t, lane][:, 0:1]
        m = jnp.maximum(m_old, jnp.max(s, axis=1, keepdims=True))
        scale = jnp.exp2(m_old - m)
        p = jnp.exp2(s - m)
        total = l_ref[t, lane][:, 0:1] * scale + jnp.sum(p, axis=1, keepdims=True)
        acc = acc_ref[t, lane] * scale + dot(p.astype(BF16), vals)
        return m, total, acc

    def keep(t, lane, state):
        m, total, acc = state
        m_ref[t, lane] = jnp.broadcast_to(m, (2 * LANE, HEAD))
        l_ref[t, lane] = jnp.broadcast_to(total, (2 * LANE, HEAD))
        acc_ref[t, lane] = acc

    def finish(h, lane, total, acc):
        att = (acc / total).astype(BF16)
        att_o[h, lane, :, 0:HEAD] = att[0:LANE]
        att_o[h, lane, :, HEAD:2 * HEAD] = att[LANE:2 * LANE]

    def sibling_keys(t):
        h = (small + t) % 2

        def one_lane(lane, carry):
            keep(t, lane, more_keys(t, h, lane, kvs[0, h], kvs[1, h]))
            return carry

        lax.fori_loop(0, LANES, one_lane, 0)

    own_keys(0)

    @pl.when(core == 1)
    def _():
        for j in range(2):
            to_sibling[j].wait_recv()
        sibling_keys(0)

    for lane in range(LANES):
        finish(small, lane, l_ref[0, lane][:, 0:1], acc_ref[0, lane])
    landed(0)
    landed(1)
    import_group(3)
    forward(0)
    forward(1)
    landed(2)
    send(att_o.at[small], att_x.at[small], ax_s.at[0], ax_r.at[LANES + 1], partner)
    up_step(2)
    own_keys(1)

    @pl.when(core == 1)
    def _():
        sibling_keys(1)

    up_step(3)
    for j in range(2):
        arrived(kvp.at[j, core], kv_r.at[j])
        send(kvp.at[j, core], kvp.at[j, core], kv_s.at[4], kv_r.at[4 + j], sibling)

    forward(2)

    def pair_keys(lane, carry):
        keep(1, lane, more_keys(1, large, lane, kvp[0, core], kvp[1, core]))
        return carry

    lax.fori_loop(0, LANES, pair_keys, 0)
    up_step(4)
    pass_on(0)
    for j in range(2):
        arrived(kvp.at[j, 1 - core], kv_r.at[4 + j])
    for lane in range(LANES):
        _, total, acc = more_keys(1, large, lane, kvp[0, 1 - core], kvp[1, 1 - core])
        finish(large, lane, total, acc)
        send(att_o.at[large, lane], att_x.at[large, lane], ax_s.at[0], ax_r.at[lane], partner)
    landed(3)
    forward(3)
    pass_on(1)

    arrived(dt_x, ax_r.at[LANES])
    arrived(att_x.at[small], ax_r.at[LANES + 1])
    arrived(up_all.at[(z + 4) % 8], up_r.at[0, 3])
    arrived(up_all.at[(z + 3) % 8], up_r.at[1, 2])
    loaded(0)
    ready(0)

    def product(i, half, own, other, low):
        cols = slice(half * HALF_COLS, (half + 1) * HALF_COLS)
        n = PIECES.index((i, half))
        up = up_all[(z + ORDER[i]) % 8, :, cols]
        out = dot(low, jnp.concatenate([up, up, up], axis=0))
        for h in range(2):
            out = out + dot(own[h], wn[i, h, :, cols]) + dot(other[h], wo[n, h])
        return out

    def operands(first, count):
        rows = slice(first, first + count)
        own = [att_o[h, rows].reshape(count * LANE, 2 * HEAD) for h in range(2)]
        other = [att_x[h, rows].reshape(count * LANE, 2 * HEAD) for h in range(2)]
        return own, other, low3[rows].reshape(count * LANE, 3 * RANK)

    for lane in range(LANES):
        arrived(att_x.at[large, lane], ax_r.at[lane])
        low = jnp.zeros((LANE, 3 * RANK), F32)
        for h in range(2):
            low = low + dot_nt(att_o[h, lane], dt_o[h]) + dot_nt(att_x[h, lane], dt_x[h])
        low = low * ADAPTER_SCALE
        top = low.astype(BF16).astype(F32)
        rest = low - top
        mid = rest.astype(BF16).astype(F32)
        third = lax.broadcasted_iota(jnp.int32, low.shape, 1) // RANK
        low3[lane] = jnp.where(third == 0, top, jnp.where(third == 1, mid, rest - mid)).astype(BF16)
        own, other, low = operands(lane, 1)
        for d in range(2):
            h0s[d, lane] = product(0, d, own, other, low).astype(BF16)
            send(h0s.at[d, lane], h0r.at[d, lane], rs_s.at[0], rs_r.at[d, lane, 0], ring[d])
        if lane == 2:
            pass_on(2)
    import_group(4)
    ready(1)
    own, other, low = operands(0, LANES)
    for d in range(2):
        start = product(STEP_CHUNK[d][1], 1 - d, own, other, low).astype(BF16)
        for lane in range(LANES):
            o1s[d, lane] = start[lane * LANE:(lane + 1) * LANE]
            send(o1s.at[d, lane], r1.at[d, lane, 1 - d], rs_s.at[2], rs_r.at[d, lane, 2], ring[d])
    ready(2)
    for d in range(2):
        i = STEP_CHUNK[d][1]
        c_ref[i, d] = product(i, d, own, other, low)
    pass_on(3)

    def whole_chunk(i):
        own, other, low = operands(0, LANES)
        for half in range(2):
            c_ref[i, half] = product(i, half, own, other, low)

    for lane in range(LANES):
        rows = slice(lane * LANE, (lane + 1) * LANE)
        for d in range(2):
            slot = h0r.at[d, lane]
            arrived(slot, rs_r.at[d, lane, 0])
            h0r[d, lane] = (h0r[d, lane].astype(F32) + c_ref[STEP_CHUNK[d][1], d, rows]).astype(BF16)
            send(slot, r1.at[d, lane, d], rs_s.at[1], rs_r.at[d, lane, 1], ring[d])
    landed(4)
    forward(4)
    loaded(1)
    ready(3)
    for i in range(3, 5):
        whole_chunk(i)

    def add_chunk(buf, d, lane, i):
        for half in range(2):
            rows = slice(lane * LANE, (lane + 1) * LANE)
            buf[d, lane, half] = (buf[d, lane, half].astype(F32) + c_ref[i, half, rows]).astype(BF16)

    for lane in range(LANES):
        for d in range(2):
            for half in range(2):
                msg = 1 if half == d else 2
                arrived(r1.at[d, lane, half], rs_r.at[d, lane, msg])
            add_chunk(r1, d, lane, STEP_CHUNK[d][2])
            send(r1.at[d, lane], r2.at[d, lane], rs_s.at[3], rs_r.at[d, lane, 3], ring[d])
    pass_on(4)
    loaded(2)
    ready(4)
    for i in range(5, 7):
        whole_chunk(i)
    for lane in range(LANES):
        for d in range(2):
            arrived(r2.at[d, lane], rs_r.at[d, lane, 3])
            add_chunk(r2, d, lane, STEP_CHUNK[d][3])
            send(r2.at[d, lane], r3.at[d, lane], rs_s.at[4], rs_r.at[d, lane, 4], ring[d])
    whole_chunk(7)
    for lane in range(LANES):
        rows = slice(lane * LANE, (lane + 1) * LANE)
        for d in range(2):
            arrived(r3.at[d, lane], rs_r.at[d, lane, 4])
        for half in range(2):
            total = c_ref[7, half, rows] + r3[0, lane, half].astype(F32) + r3[1, lane, half].astype(F32)
            out_ref[rows, half * HALF_COLS:(half + 1) * HALF_COLS] = total.astype(BF16)

    for n, buf in enumerate((h0s, h0r, o1s, r1, r2)):
        left(buf, rs_s.at[n])
    part = wo.at[:, 0, 0:64]
    left(part, wx_s.at[0])
    for k in range(1, 4):
        left(part, wy_s.at[k - 1])
    for k in range(4):
        left(part, ws_s.at[k])
    left(up_all.at[0:7], up_s.at[0])
    left(att_o, ax_s.at[0])
    left(dt_o, ax_s.at[0])
    for j in range(2):
        left(kvp.at[j, 0], kv_s.at[j])
    left(kvp.at[:, 0], kv_s.at[4])

    @pl.when(core == 0)
    def _():
        for one in to_sibling:
            one.wait_send()


def body(queries, keys, values, output_matrix, adapter_down_weight, adapter_up_weight):
    vmem = pl.BlockSpec(memory_space=pltpu.VMEM)
    hbm = pl.BlockSpec(memory_space=pl.ANY)
    dma = pltpu.SemaphoreType.DMA
    return pl.pallas_call(
        kernel,
        out_shape=jax.ShapeDtypeStruct((ROWS, COLS), BF16),
        in_specs=[vmem, hbm, hbm, hbm, vmem, vmem],
        out_specs=vmem,
        scratch_shapes=[
            pltpu.VMEM((2, 2, ROWS, HEAD), BF16),
            pltpu.VMEM((2, 2, ROWS, HEAD), BF16),
            pltpu.VMEM((2, 2, ROWS, HEAD), BF16),
            pltpu.VMEM((8, 2, 256, COLS), BF16),
            pltpu.VMEM((16, 2, 256, HALF_COLS), BF16),
            pltpu.VMEM((2, LANES, LANE, 256), BF16),
            pltpu.VMEM((2, LANES, LANE, 256), BF16),
            pltpu.VMEM((2, 3 * RANK, 256), BF16),
            pltpu.VMEM((2, 3 * RANK, 256), BF16),
            pltpu.VMEM((8, RANK, COLS), BF16),
            pltpu.VMEM((LANES, LANE, 3 * RANK), BF16),
            pltpu.VMEM((2, LANES, 2 * LANE, HEAD), F32),
            pltpu.VMEM((2, LANES, 2 * LANE, HEAD), F32),
            pltpu.VMEM((2, LANES, 2 * LANE, HEAD), F32),
            pltpu.VMEM((8, 2, ROWS, HALF_COLS), F32),
            pltpu.VMEM((2, LANES, LANE, HALF_COLS), BF16),
            pltpu.VMEM((2, LANES, LANE, HALF_COLS), BF16),
            pltpu.VMEM((2, LANES, LANE, HALF_COLS), BF16),
            pltpu.VMEM((2, LANES, 2, LANE, HALF_COLS), BF16),
            pltpu.VMEM((2, LANES, 2, LANE, HALF_COLS), BF16),
            pltpu.VMEM((2, LANES, 2, LANE, HALF_COLS), BF16),
            dma((2,)), dma((3,)),
            dma((5,)), dma((6,)),
            dma((1,)), dma((2, 4)),
            dma((1,)), dma((LANES + 2,)),
            dma((1,)), dma((5,)),
            dma((3,)), dma((5, 3)),
            dma((4,)), dma((5, 4)),
            dma((5,)), dma((2, LANES, 5)),
        ],
        compiler_params=pltpu.CompilerParams(
            collective_id=0, has_side_effects=True, vmem_limit_bytes=56 * 2**20
        ),
        cost_estimate=pl.CostEstimate(flops=6 * 10**9, bytes_accessed=12 * 2**20, transcendentals=3 * 10**6),
        name="attend_and_project",
    )(queries, keys, values, output_matrix, jnp.swapaxes(adapter_down_weight, 1, 2), adapter_up_weight)


def solution(mesh):
    return jax.shard_map(
        body,
        mesh=mesh,
        in_specs=(
            P(None, "ctx", "tp"),
            P(None, "ctx", None),
            P(None, "ctx", None),
            P(None, "tp", None),
            P(None, "tp", None),
            P(None, "tp"),
        ),
        out_specs=P("ctx", "tp"),
        check_vma=False,
    )
```

```python
import functools
import math

import jax
import jax.numpy as jnp
from jax import lax
from jax.experimental import pallas as pl
from jax.experimental.pallas import tpu as pltpu
from jax.sharding import PartitionSpec as P

HEAD = 128
ROWS = 512
LANES = 4
LANE = 128
RANK = 16
COLS = 512
HALF_COLS = 256
ADAPTER_SCALE = 2.0
SCORE_SCALE = math.log2(math.e) / math.sqrt(HEAD)
MESH = pl.DeviceIdType.MESH
F32 = jnp.float32
BF16 = jnp.bfloat16

ORDER = (4, 3, 5, 2, 6, 1, 7, 0)
PIECES = ((0, 0), (0, 1), (1, 1), (2, 0), (1, 0), (2, 1)) + tuple((i, half) for i in range(3, 8) for half in range(2))
GROUPS = ((0, 2), (2, 2), (4, 2), (6, 4), (10, 6))
STEP_CHUNK = ((0, 1, 3, 5, 7), (0, 2, 4, 6, 7))


def dot(a, b):
    return jnp.dot(a, b, preferred_element_type=F32)


def dot_nt(a, b):
    return lax.dot_general(a, b, (((1,), (1,)), ((), ())), preferred_element_type=F32)


def kernel(
    q_ref, k_hbm, v_hbm, w_hbm, down_ref, up_ref, out_ref,
    kvo, kvs, kvp, wn, wo, att_o, att_x, dt_o, dt_x, up_all, low3,
    m_ref, l_ref, acc_ref, c_ref, h0s, h0r, o1s, r1, r2, r3,
    loc_sem, wn_sem, kv_s, kv_r, up_s, up_r, ax_s, ax_r,
    wx_s, wx_r, wy_s, wy_r, ws_s, ws_r, rs_s, rs_r,
):
    ctx = lax.axis_index("ctx")
    tp = lax.axis_index("tp")
    core = ctx % 2
    y = (ctx // 2) % 4
    x_lo = ctx // 8
    z = tp % 8
    x_hi = tp // 8

    def at_z(k):
        return (ctx, x_hi * 8 + (z + k) % 8)

    def at_y(k):
        return ((x_lo * 4 + (y + k) % 4) * 2 + core, tp)

    sibling = (x_lo * 8 + y * 2 + 1 - core, tp)
    nxt = ((ctx + 2) % 16, tp)
    prv = ((ctx + 14) % 16, tp)
    partner = (ctx, (1 - x_hi) * 8 + z)
    w_partner = ((1 - x_lo) * 8 + y * 2 + core, (1 - x_hi) * 8 + z)

    def copy(src, dst, ss, rs, dev):
        return pltpu.make_async_remote_copy(
            src_ref=src, dst_ref=dst, send_sem=ss, recv_sem=rs, device_id=dev, device_id_type=MESH
        )

    def send(src, dst, ss, rs, dev):
        copy(src, dst, ss, rs, dev).start()

    def arrived(dst, rs):
        copy(dst, dst, kv_s.at[0], rs, sibling).wait_recv()

    def left(src, ss):
        copy(src, src, ss, kv_r.at[0], sibling).wait_send()

    kv_col = pl.ds(pl.multiple_of((tp // 4) * HEAD, HEAD), HEAD)
    load_k = pltpu.make_async_copy(k_hbm.at[:, :, kv_col], kvo.at[0], loc_sem.at[0])
    load_v = pltpu.make_async_copy(v_hbm.at[:, :, kv_col], kvo.at[1], loc_sem.at[1])
    load_k.start()
    load_v.start()

    def col_of(hi, i, half=0, width=COLS):
        first = (hi * 8 + (z + ORDER[i]) % 8) * COLS + half * HALF_COLS
        return pl.ds(pl.multiple_of(first, width), width)

    barrier = pltpu.get_barrier_semaphore()
    friends = [sibling, nxt, prv, partner, w_partner]
    friends += [at_y(k) for k in range(1, 4)] + [at_z(1), at_z(7)]
    for friend in friends:
        pl.semaphore_signal(barrier, inc=1, device_id=friend, device_id_type=MESH)

    for h in range(2):
        dt_o[h] = jnp.concatenate([down_ref[h]] * 3, axis=0)
    up_all[z] = up_ref[...]

    pl.semaphore_wait(barrier, len(friends))

    w_half = y // 2

    def rows_of(who_y, who_core):
        return pl.ds(pl.multiple_of(((who_y % 2) * 2 + who_core) * 64, 64), 64)

    def import_group(g):
        first, count = GROUPS[g]
        for n in range(first, first + count):
            send(
                w_hbm.at[w_half, rows_of(y, core), col_of(1 - x_hi, *PIECES[n], HALF_COLS)],
                wo.at[n, w_half, rows_of(y, core)],
                wx_s.at[0], wx_r.at[g], w_partner,
            )

    def group(g, half, rows):
        first, count = GROUPS[g]
        return wo.at[pl.ds(first, count), half, rows]

    def landed(g):
        arrived(group(g, w_half, rows_of(y, core)), wx_r.at[g])

    def forward(g):
        mine = group(g, w_half, rows_of(y, core))
        for k in range(1, 4):
            send(mine, mine, wy_s.at[k - 1], wy_r.at[g, k - 1], at_y(k))
        send(mine, mine, ws_s.at[0], ws_r.at[g, 0], sibling)

    def pass_on(g):
        for k in range(1, 4):
            other = (y + 4 - k) % 4
            part = group(g, other // 2, rows_of(other, core))
            arrived(part, wy_r.at[g, k - 1])
            send(part, part, ws_s.at[k], ws_r.at[g, k], sibling)

    def ready(g):
        for k in range(4):
            other = (y + 4 - k) % 4
            arrived(group(g, other // 2, rows_of(other, 1 - core)), ws_r.at[g, k])

    def up_step(k):
        for d in range(2):
            if k == 4 and d == 1:
                continue
            slot = up_all.at[(z + (9 - k if d == 0 else k - 1)) % 8]
            if k > 1:
                arrived(slot, up_r.at[d, k - 2])
            send(slot, slot, up_s.at[0], up_r.at[d, k - 1], ring[d])

    ring = (at_z(1), at_z(7))
    small = y % 2
    large = 1 - small
    kv = (k_hbm, v_hbm)
    for j in range(2):
        send(kv[j].at[small, :, kv_col], kvp.at[j, core], kv_s.at[j], kv_r.at[j], nxt)
    for g in range(3):
        import_group(g)
    to_sibling = [
        copy(kv[j].at[:, :, kv_col], kvs.at[j], kv_s.at[2 + j], kv_r.at[2 + j], sibling)
        for j in range(2)
    ]

    @pl.when(core == 0)
    def _():
        for one in to_sibling:
            one.start()

    send(dt_o, dt_x, ax_s.at[0], ax_r.at[LANES], partner)

    up_step(1)

    load_w = [
        pltpu.make_async_copy(w_hbm.at[:, :, col_of(x_hi, i)], wn.at[i], wn_sem.at[i // 3]) for i in range(8)
    ]
    for one in load_w:
        one.start()

    def loaded(n):
        part = wn.at[3 * n:min(3 * n + 3, 8)]
        pltpu.make_async_copy(part, part, wn_sem.at[n]).wait()

    load_k.wait()
    load_v.wait()

    def queries_of(h, lane):
        rows = pl.ds(pl.multiple_of(lane * LANE, LANE), LANE)
        return jnp.concatenate([q_ref[h, rows, 0:HEAD], q_ref[h, rows, HEAD:2 * HEAD]], axis=0)

    def own_keys(t):
        h = (small + t) % 2
        for lane in range(LANES):
            q = queries_of(h, lane)
            edge = lane * LANE
            s1 = dot_nt(q, kvo[0, h, edge:edge + LANE, :]) * SCORE_SCALE
            row = lax.broadcasted_iota(jnp.int32, s1.shape, 0) % LANE
            col = lax.broadcasted_iota(jnp.int32, s1.shape, 1)
            s1 = jnp.where(col <= row, s1, -jnp.inf)
            m = jnp.max(s1, axis=1, keepdims=True)
            if lane:
                s0 = dot_nt(q, kvo[0, h, 0:edge, :]) * SCORE_SCALE
                m = jnp.maximum(m, jnp.max(s0, axis=1, keepdims=True))
            p1 = jnp.exp2(s1 - m)
            total = jnp.sum(p1, axis=1, keepdims=True)
            acc = dot(p1.astype(BF16), kvo[1, h, edge:edge + LANE, :])
            if lane:
                p0 = jnp.exp2(s0 - m)
                total = total + jnp.sum(p0, axis=1, keepdims=True)
                acc = acc + dot(p0.astype(BF16), kvo[1, h, 0:edge, :])
            m_ref[t, lane] = jnp.broadcast_to(m, (2 * LANE, HEAD))
            l_ref[t, lane] = jnp.broadcast_to(total, (2 * LANE, HEAD))
            acc_ref[t, lane] = acc

    def more_keys(t, h, lane, keys, vals):
        s = dot_nt(queries_of(h, lane), keys) * SCORE_SCALE
        m_old = m_ref[t, lane][:, 0:1]
        m = jnp.maximum(m_old, jnp.max(s, axis=1, keepdims=True))
        scale = jnp.exp2(m_old - m)
        p = jnp.exp2(s - m)
        total = l_ref[t, lane][:, 0:1] * scale + jnp.sum(p, axis=1, keepdims=True)
        acc = acc_ref[t, lane] * scale + dot(p.astype(BF16), vals)
        return m, total, acc

    def keep(t, lane, state):
        m, total, acc = state
        m_ref[t, lane] = jnp.broadcast_to(m, (2 * LANE, HEAD))
        l_ref[t, lane] = jnp.broadcast_to(total, (2 * LANE, HEAD))
        acc_ref[t, lane] = acc

    def finish(h, lane, total, acc):
        att = (acc / total).astype(BF16)
        att_o[h, lane, :, 0:HEAD] = att[0:LANE]
        att_o[h, lane, :, HEAD:2 * HEAD] = att[LANE:2 * LANE]

    def sibling_keys(t):
        h = (small + t) % 2

        def one_lane(lane, carry):
            keep(t, lane, more_keys(t, h, lane, kvs[0, h], kvs[1, h]))
            return carry

        lax.fori_loop(0, LANES, one_lane, 0)

    own_keys(0)

    @pl.when(core == 1)
    def _():
        for j in range(2):
            to_sibling[j].wait_recv()
        sibling_keys(0)

    for lane in range(LANES):
        finish(small, lane, l_ref[0, lane][:, 0:1], acc_ref[0, lane])
    landed(0)
    landed(1)
    import_group(3)
    forward(0)
    forward(1)
    landed(2)
    send(att_o.at[small], att_x.at[small], ax_s.at[0], ax_r.at[LANES + 1], partner)
    up_step(2)
    own_keys(1)

    @pl.when(core == 1)
    def _():
        sibling_keys(1)

    up_step(3)
    for j in range(2):
        arrived(kvp.at[j, core], kv_r.at[j])
        send(kvp.at[j, core], kvp.at[j, core], kv_s.at[4], kv_r.at[4 + j], sibling)

    forward(2)

    def pair_keys(lane, carry):
        keep(1, lane, more_keys(1, large, lane, kvp[0, core], kvp[1, core]))
        return carry

    lax.fori_loop(0, LANES, pair_keys, 0)
    up_step(4)
    pass_on(0)
    for j in range(2):
        arrived(kvp.at[j, 1 - core], kv_r.at[4 + j])
    for lane in range(LANES):
        _, total, acc = more_keys(1, large, lane, kvp[0, 1 - core], kvp[1, 1 - core])
        finish(large, lane, total, acc)
        send(att_o.at[large, lane], att_x.at[large, lane], ax_s.at[0], ax_r.at[lane], partner)
    pass_on(1)

    arrived(dt_x, ax_r.at[LANES])
    arrived(att_x.at[small], ax_r.at[LANES + 1])
    arrived(up_all.at[(z + 4) % 8], up_r.at[0, 3])
    arrived(up_all.at[(z + 3) % 8], up_r.at[1, 2])
    loaded(0)
    ready(0)

    def product(i, half, own, other, low):
        cols = slice(half * HALF_COLS, (half + 1) * HALF_COLS)
        n = PIECES.index((i, half))
        up = up_all[(z + ORDER[i]) % 8, :, cols]
        out = dot(low, jnp.concatenate([up, up, up], axis=0))
        for h in range(2):
            out = out + dot(own[h], wn[i, h, :, cols]) + dot(other[h], wo[n, h])
        return out

    def operands(first, count):
        rows = slice(first, first + count)
        own = [att_o[h, rows].reshape(count * LANE, 2 * HEAD) for h in range(2)]
        other = [att_x[h, rows].reshape(count * LANE, 2 * HEAD) for h in range(2)]
        return own, other, low3[rows].reshape(count * LANE, 3 * RANK)

    for lane in range(LANES):
        arrived(att_x.at[large, lane], ax_r.at[lane])
        low = jnp.zeros((LANE, 3 * RANK), F32)
        for h in range(2):
            low = low + dot_nt(att_o[h, lane], dt_o[h]) + dot_nt(att_x[h, lane], dt_x[h])
        low = low * ADAPTER_SCALE
        top = low.astype(BF16).astype(F32)
        rest = low - top
        mid = rest.astype(BF16).astype(F32)
        third = lax.broadcasted_iota(jnp.int32, low.shape, 1) // RANK
        low3[lane] = jnp.where(third == 0, top, jnp.where(third == 1, mid, rest - mid)).astype(BF16)
        own, other, low = operands(lane, 1)
        for d in range(2):
            h0s[d, lane] = product(0, d, own, other, low).astype(BF16)
            send(h0s.at[d, lane], h0r.at[d, lane], rs_s.at[0], rs_r.at[d, lane, 0], ring[d])
        if lane == 0:
            landed(3)
            forward(3)
        if lane == 2:
            pass_on(2)
    import_group(4)
    ready(1)
    own, other, low = operands(0, LANES)
    for d in range(2):
        start = product(STEP_CHUNK[d][1], 1 - d, own, other, low).astype(BF16)
        for lane in range(LANES):
            o1s[d, lane] = start[lane * LANE:(lane + 1) * LANE]
            send(o1s.at[d, lane], r1.at[d, lane, 1 - d], rs_s.at[2], rs_r.at[d, lane, 2], ring[d])
    ready(2)
    for d in range(2):
        i = STEP_CHUNK[d][1]
        c_ref[i, d] = product(i, d, own, other, low)

    def whole_chunk(i):
        own, other, low = operands(0, LANES)
        for half in range(2):
            c_ref[i, half] = product(i, half, own, other, low)

    for lane in range(LANES):
        rows = slice(lane * LANE, (lane + 1) * LANE)
        for d in range(2):
            slot = h0r.at[d, lane]
            arrived(slot, rs_r.at[d, lane, 0])
            h0r[d, lane] = (h0r[d, lane].astype(F32) + c_ref[STEP_CHUNK[d][1], d, rows]).astype(BF16)
            send(slot, r1.at[d, lane, d], rs_s.at[1], rs_r.at[d, lane, 1], ring[d])
        if lane == 1:
            pass_on(3)
    landed(4)
    forward(4)
    loaded(1)
    ready(3)
    for i in range(3, 5):
        whole_chunk(i)

    def add_chunk(buf, d, lane, i):
        for half in range(2):
            rows = slice(lane * LANE, (lane + 1) * LANE)
            buf[d, lane, half] = (buf[d, lane, half].astype(F32) + c_ref[i, half, rows]).astype(BF16)

    for lane in range(LANES):
        for d in range(2):
            for half in range(2):
                msg = 1 if half == d else 2
                arrived(r1.at[d, lane, half], rs_r.at[d, lane, msg])
            add_chunk(r1, d, lane, STEP_CHUNK[d][2])
            send(r1.at[d, lane], r2.at[d, lane], rs_s.at[3], rs_r.at[d, lane, 3], ring[d])
    pass_on(4)
    loaded(2)
    ready(4)
    for i in range(5, 7):
        whole_chunk(i)
    for lane in range(LANES):
        for d in range(2):
            arrived(r2.at[d, lane], rs_r.at[d, lane, 3])
            add_chunk(r2, d, lane, STEP_CHUNK[d][3])
            send(r2.at[d, lane], r3.at[d, lane], rs_s.at[4], rs_r.at[d, lane, 4], ring[d])
    whole_chunk(7)
    for lane in range(LANES):
        rows = slice(lane * LANE, (lane + 1) * LANE)
        for d in range(2):
            arrived(r3.at[d, lane], rs_r.at[d, lane, 4])
        for half in range(2):
            total = c_ref[7, half, rows] + r3[0, lane, half].astype(F32) + r3[1, lane, half].astype(F32)
            out_ref[rows, half * HALF_COLS:(half + 1) * HALF_COLS] = total.astype(BF16)

    for n, buf in enumerate((h0s, h0r, o1s, r1, r2)):
        left(buf, rs_s.at[n])
    part = wo.at[:, 0, 0:64]
    left(part, wx_s.at[0])
    for k in range(1, 4):
        left(part, wy_s.at[k - 1])
    for k in range(4):
        left(part, ws_s.at[k])
    left(up_all.at[0:7], up_s.at[0])
    left(att_o, ax_s.at[0])
    left(dt_o, ax_s.at[0])
    for j in range(2):
        left(kvp.at[j, 0], kv_s.at[j])
    left(kvp.at[:, 0], kv_s.at[4])

    @pl.when(core == 0)
    def _():
        for one in to_sibling:
            one.wait_send()


def body(queries, keys, values, output_matrix, adapter_down_weight, adapter_up_weight):
    vmem = pl.BlockSpec(memory_space=pltpu.VMEM)
    hbm = pl.BlockSpec(memory_space=pl.ANY)
    dma = pltpu.SemaphoreType.DMA
    return pl.pallas_call(
        kernel,
        out_shape=jax.ShapeDtypeStruct((ROWS, COLS), BF16),
        in_specs=[vmem, hbm, hbm, hbm, vmem, vmem],
        out_specs=vmem,
        scratch_shapes=[
            pltpu.VMEM((2, 2, ROWS, HEAD), BF16),
            pltpu.VMEM((2, 2, ROWS, HEAD), BF16),
            pltpu.VMEM((2, 2, ROWS, HEAD), BF16),
            pltpu.VMEM((8, 2, 256, COLS), BF16),
            pltpu.VMEM((16, 2, 256, HALF_COLS), BF16),
            pltpu.VMEM((2, LANES, LANE, 256), BF16),
            pltpu.VMEM((2, LANES, LANE, 256), BF16),
            pltpu.VMEM((2, 3 * RANK, 256), BF16),
            pltpu.VMEM((2, 3 * RANK, 256), BF16),
            pltpu.VMEM((8, RANK, COLS), BF16),
            pltpu.VMEM((LANES, LANE, 3 * RANK), BF16),
            pltpu.VMEM((2, LANES, 2 * LANE, HEAD), F32),
            pltpu.VMEM((2, LANES, 2 * LANE, HEAD), F32),
            pltpu.VMEM((2, LANES, 2 * LANE, HEAD), F32),
            pltpu.VMEM((8, 2, ROWS, HALF_COLS), F32),
            pltpu.VMEM((2, LANES, LANE, HALF_COLS), BF16),
            pltpu.VMEM((2, LANES, LANE, HALF_COLS), BF16),
            pltpu.VMEM((2, LANES, LANE, HALF_COLS), BF16),
            pltpu.VMEM((2, LANES, 2, LANE, HALF_COLS), BF16),
            pltpu.VMEM((2, LANES, 2, LANE, HALF_COLS), BF16),
            pltpu.VMEM((2, LANES, 2, LANE, HALF_COLS), BF16),
            dma((2,)), dma((3,)),
            dma((5,)), dma((6,)),
            dma((1,)), dma((2, 4)),
            dma((1,)), dma((LANES + 2,)),
            dma((1,)), dma((5,)),
            dma((3,)), dma((5, 3)),
            dma((4,)), dma((5, 4)),
            dma((5,)), dma((2, LANES, 5)),
        ],
        compiler_params=pltpu.CompilerParams(
            collective_id=0, has_side_effects=True, vmem_limit_bytes=56 * 2**20
        ),
        cost_estimate=pl.CostEstimate(flops=6 * 10**9, bytes_accessed=12 * 2**20, transcendentals=3 * 10**6),
        name="attend_and_project",
    )(queries, keys, values, output_matrix, jnp.swapaxes(adapter_down_weight, 1, 2), adapter_up_weight)


def solution(mesh):
    return jax.shard_map(
        body,
        mesh=mesh,
        in_specs=(
            P(None, "ctx", "tp"),
            P(None, "ctx", None),
            P(None, "ctx", None),
            P(None, "tp", None),
            P(None, "tp", None),
            P(None, "tp"),
        ),
        out_specs=P("ctx", "tp"),
        check_vma=False,
    )
```

```python
import functools
import math

import jax
import jax.numpy as jnp
from jax import lax
from jax.experimental import pallas as pl
from jax.experimental.pallas import tpu as pltpu
from jax.sharding import PartitionSpec as P

HEAD = 128
ROWS = 512
LANES = 4
LANE = 128
RANK = 16
COLS = 512
HALF_COLS = 256
ADAPTER_SCALE = 2.0
SCORE_SCALE = math.log2(math.e) / math.sqrt(HEAD)
MESH = pl.DeviceIdType.MESH
F32 = jnp.float32
BF16 = jnp.bfloat16

ORDER = (4, 3, 5, 2, 6, 1, 7, 0)
PIECES = ((0, 0), (0, 1), (1, 1), (2, 0), (1, 0), (2, 1)) + tuple((i, half) for i in range(3, 8) for half in range(2))
GROUPS = ((0, 2), (2, 2), (4, 2), (6, 4), (10, 6))
STEP_CHUNK = ((0, 1, 3, 5, 7), (0, 2, 4, 6, 7))


def dot(a, b):
    return jnp.dot(a, b, preferred_element_type=F32)


def dot_nt(a, b):
    return lax.dot_general(a, b, (((1,), (1,)), ((), ())), preferred_element_type=F32)


def kernel(
    q_ref, k_hbm, v_hbm, w_hbm, down_ref, up_ref, out_ref,
    kvo, kvs, kvp, wn, wo, att_o, att_x, dt_o, dt_x, up_all, low3,
    m_ref, l_ref, acc_ref, c_ref, h0s, h0r, o1s, r1, r2, r3,
    loc_sem, wn_sem, kv_s, kv_r, up_s, up_r, ax_s, ax_r,
    wx_s, wx_r, wy_s, wy_r, ws_s, ws_r, rs_s, rs_r,
):
    ctx = lax.axis_index("ctx")
    tp = lax.axis_index("tp")
    core = ctx % 2
    y = (ctx // 2) % 4
    x_lo = ctx // 8
    z = tp % 8
    x_hi = tp // 8

    def at_z(k):
        return (ctx, x_hi * 8 + (z + k) % 8)

    def at_y(k):
        return ((x_lo * 4 + (y + k) % 4) * 2 + core, tp)

    sibling = (x_lo * 8 + y * 2 + 1 - core, tp)
    nxt = ((ctx + 2) % 16, tp)
    prv = ((ctx + 14) % 16, tp)
    partner = (ctx, (1 - x_hi) * 8 + z)
    w_partner = ((1 - x_lo) * 8 + y * 2 + core, (1 - x_hi) * 8 + z)

    def copy(src, dst, ss, rs, dev):
        return pltpu.make_async_remote_copy(
            src_ref=src, dst_ref=dst, send_sem=ss, recv_sem=rs, device_id=dev, device_id_type=MESH
        )

    def send(src, dst, ss, rs, dev):
        copy(src, dst, ss, rs, dev).start()

    def arrived(dst, rs):
        copy(dst, dst, kv_s.at[0], rs, sibling).wait_recv()

    def left(src, ss):
        copy(src, src, ss, kv_r.at[0], sibling).wait_send()

    kv_col = pl.ds(pl.multiple_of((tp // 4) * HEAD, HEAD), HEAD)
    load_k = pltpu.make_async_copy(k_hbm.at[:, :, kv_col], kvo.at[0], loc_sem.at[0])
    load_v = pltpu.make_async_copy(v_hbm.at[:, :, kv_col], kvo.at[1], loc_sem.at[1])
    load_k.start()
    load_v.start()

    def col_of(hi, i, half=0, width=COLS):
        first = (hi * 8 + (z + ORDER[i]) % 8) * COLS + half * HALF_COLS
        return pl.ds(pl.multiple_of(first, width), width)

    barrier = pltpu.get_barrier_semaphore()
    friends = [sibling, nxt, prv, partner, w_partner]
    friends += [at_y(k) for k in range(1, 4)] + [at_z(1), at_z(7)]
    for friend in friends:
        pl.semaphore_signal(barrier, inc=1, device_id=friend, device_id_type=MESH)

    for h in range(2):
        dt_o[h] = jnp.concatenate([down_ref[h]] * 3, axis=0)
    up_all[z] = up_ref[...]

    pl.semaphore_wait(barrier, len(friends))

    w_half = y // 2

    def rows_of(who_y, who_core):
        return pl.ds(pl.multiple_of(((who_y % 2) * 2 + who_core) * 64, 64), 64)

    def import_group(g):
        first, count = GROUPS[g]
        for n in range(first, first + count):
            send(
                w_hbm.at[w_half, rows_of(y, core), col_of(1 - x_hi, *PIECES[n], HALF_COLS)],
                wo.at[n, w_half, rows_of(y, core)],
                wx_s.at[0], wx_r.at[g], w_partner,
            )

    def group(g, half, rows):
        first, count = GROUPS[g]
        return wo.at[pl.ds(first, count), half, rows]

    def landed(g):
        arrived(group(g, w_half, rows_of(y, core)), wx_r.at[g])

    def forward(g):
        mine = group(g, w_half, rows_of(y, core))
        for k in range(1, 4):
            send(mine, mine, wy_s.at[k - 1], wy_r.at[g, k - 1], at_y(k))
        send(mine, mine, ws_s.at[0], ws_r.at[g, 0], sibling)

    def pass_on(g):
        for k in range(1, 4):
            other = (y + 4 - k) % 4
            part = group(g, other // 2, rows_of(other, core))
            arrived(part, wy_r.at[g, k - 1])
            send(part, part, ws_s.at[k], ws_r.at[g, k], sibling)

    def ready(g):
        for k in range(4):
            other = (y + 4 - k) % 4
            arrived(group(g, other // 2, rows_of(other, 1 - core)), ws_r.at[g, k])

    def up_step(k):
        for d in range(2):
            if k == 4 and d == 1:
                continue
            slot = up_all.at[(z + (9 - k if d == 0 else k - 1)) % 8]
            if k > 1:
                arrived(slot, up_r.at[d, k - 2])
            send(slot, slot, up_s.at[0], up_r.at[d, k - 1], ring[d])

    ring = (at_z(1), at_z(7))
    small = y % 2
    large = 1 - small
    kv = (k_hbm, v_hbm)
    for j in range(2):
        send(kv[j].at[small, :, kv_col], kvp.at[j, core], kv_s.at[j], kv_r.at[j], nxt)
    for g in range(3):
        import_group(g)
    to_sibling = [
        copy(kv[j].at[:, :, kv_col], kvs.at[j], kv_s.at[2 + j], kv_r.at[2 + j], sibling)
        for j in range(2)
    ]

    @pl.when(core == 0)
    def _():
        for one in to_sibling:
            one.start()

    send(dt_o, dt_x, ax_s.at[0], ax_r.at[LANES], partner)

    up_step(1)

    load_w = [
        pltpu.make_async_copy(w_hbm.at[:, :, col_of(x_hi, i)], wn.at[i], wn_sem.at[i // 3]) for i in range(8)
    ]
    for one in load_w:
        one.start()

    def loaded(n):
        part = wn.at[3 * n:min(3 * n + 3, 8)]
        pltpu.make_async_copy(part, part, wn_sem.at[n]).wait()

    load_k.wait()
    load_v.wait()

    def queries_of(h, lane):
        rows = pl.ds(pl.multiple_of(lane * LANE, LANE), LANE)
        return jnp.concatenate([q_ref[h, rows, 0:HEAD], q_ref[h, rows, HEAD:2 * HEAD]], axis=0)

    def own_keys(t):
        h = (small + t) % 2
        for lane in range(LANES):
            q = queries_of(h, lane)
            edge = lane * LANE
            s1 = dot_nt(q, kvo[0, h, edge:edge + LANE, :]) * SCORE_SCALE
            row = lax.broadcasted_iota(jnp.int32, s1.shape, 0) % LANE
            col = lax.broadcasted_iota(jnp.int32, s1.shape, 1)
            s1 = jnp.where(col <= row, s1, -jnp.inf)
            m = jnp.max(s1, axis=1, keepdims=True)
            if lane:
                s0 = dot_nt(q, kvo[0, h, 0:edge, :]) * SCORE_SCALE
                m = jnp.maximum(m, jnp.max(s0, axis=1, keepdims=True))
            p1 = jnp.exp2(s1 - m)
            total = jnp.sum(p1, axis=1, keepdims=True)
            acc = dot(p1.astype(BF16), kvo[1, h, edge:edge + LANE, :])
            if lane:
                p0 = jnp.exp2(s0 - m)
                total = total + jnp.sum(p0, axis=1, keepdims=True)
                acc = acc + dot(p0.astype(BF16), kvo[1, h, 0:edge, :])
            m_ref[t, lane] = jnp.broadcast_to(m, (2 * LANE, HEAD))
            l_ref[t, lane] = jnp.broadcast_to(total, (2 * LANE, HEAD))
            acc_ref[t, lane] = acc

    def more_keys(t, h, lane, keys, vals):
        s = dot_nt(queries_of(h, lane), keys) * SCORE_SCALE
        m_old = m_ref[t, lane][:, 0:1]
        m = jnp.maximum(m_old, jnp.max(s, axis=1, keepdims=True))
        scale = jnp.exp2(m_old - m)
        p = jnp.exp2(s - m)
        total = l_ref[t, lane][:, 0:1] * scale + jnp.sum(p, axis=1, keepdims=True)
        acc = acc_ref[t, lane] * scale + dot(p.astype(BF16), vals)
        return m, total, acc

    def keep(t, lane, state):
        m, total, acc = state
        m_ref[t, lane] = jnp.broadcast_to(m, (2 * LANE, HEAD))
        l_ref[t, lane] = jnp.broadcast_to(total, (2 * LANE, HEAD))
        acc_ref[t, lane] = acc

    def finish(h, lane, total, acc):
        att = (acc / total).astype(BF16)
        att_o[h, lane, :, 0:HEAD] = att[0:LANE]
        att_o[h, lane, :, HEAD:2 * HEAD] = att[LANE:2 * LANE]

    def sibling_keys(t):
        h = (small + t) % 2

        def one_lane(lane, carry):
            keep(t, lane, more_keys(t, h, lane, kvs[0, h], kvs[1, h]))
            return carry

        lax.fori_loop(0, LANES, one_lane, 0)

    own_keys(0)

    @pl.when(core == 1)
    def _():
        for j in range(2):
            to_sibling[j].wait_recv()
        sibling_keys(0)

    for lane in range(LANES):
        finish(small, lane, l_ref[0, lane][:, 0:1], acc_ref[0, lane])
    landed(0)
    landed(1)
    forward(0)
    forward(1)
    landed(2)
    send(att_o.at[small], att_x.at[small], ax_s.at[0], ax_r.at[LANES + 1], partner)
    up_step(2)
    own_keys(1)

    @pl.when(core == 1)
    def _():
        sibling_keys(1)

    up_step(3)
    for j in range(2):
        arrived(kvp.at[j, core], kv_r.at[j])
        send(kvp.at[j, core], kvp.at[j, core], kv_s.at[4], kv_r.at[4 + j], sibling)

    forward(2)

    def pair_keys(lane, carry):
        keep(1, lane, more_keys(1, large, lane, kvp[0, core], kvp[1, core]))
        return carry

    lax.fori_loop(0, LANES, pair_keys, 0)
    up_step(4)
    pass_on(0)
    for j in range(2):
        arrived(kvp.at[j, 1 - core], kv_r.at[4 + j])
    for lane in range(LANES):
        _, total, acc = more_keys(1, large, lane, kvp[0, 1 - core], kvp[1, 1 - core])
        finish(large, lane, total, acc)
        send(att_o.at[large, lane], att_x.at[large, lane], ax_s.at[0], ax_r.at[lane], partner)
    pass_on(1)

    arrived(dt_x, ax_r.at[LANES])
    arrived(att_x.at[small], ax_r.at[LANES + 1])
    arrived(up_all.at[(z + 4) % 8], up_r.at[0, 3])
    arrived(up_all.at[(z + 3) % 8], up_r.at[1, 2])
    loaded(0)
    ready(0)

    def product(i, half, own, other, low):
        cols = slice(half * HALF_COLS, (half + 1) * HALF_COLS)
        n = PIECES.index((i, half))
        up = up_all[(z + ORDER[i]) % 8, :, cols]
        out = dot(low, jnp.concatenate([up, up, up], axis=0))
        for h in range(2):
            out = out + dot(own[h], wn[i, h, :, cols]) + dot(other[h], wo[n, h])
        return out

    def operands(first, count):
        rows = slice(first, first + count)
        own = [att_o[h, rows].reshape(count * LANE, 2 * HEAD) for h in range(2)]
        other = [att_x[h, rows].reshape(count * LANE, 2 * HEAD) for h in range(2)]
        return own, other, low3[rows].reshape(count * LANE, 3 * RANK)

    for lane in range(LANES):
        arrived(att_x.at[large, lane], ax_r.at[lane])
        low = jnp.zeros((LANE, 3 * RANK), F32)
        for h in range(2):
            low = low + dot_nt(att_o[h, lane], dt_o[h]) + dot_nt(att_x[h, lane], dt_x[h])
        low = low * ADAPTER_SCALE
        top = low.astype(BF16).astype(F32)
        rest = low - top
        mid = rest.astype(BF16).astype(F32)
        third = lax.broadcasted_iota(jnp.int32, low.shape, 1) // RANK
        low3[lane] = jnp.where(third == 0, top, jnp.where(third == 1, mid, rest - mid)).astype(BF16)
        own, other, low = operands(lane, 1)
        for d in range(2):
            h0s[d, lane] = product(0, d, own, other, low).astype(BF16)
            send(h0s.at[d, lane], h0r.at[d, lane], rs_s.at[0], rs_r.at[d, lane, 0], ring[d])
        if lane == 0:
            import_group(3)
        if lane == 2:
            pass_on(2)
    ready(1)
    own, other, low = operands(0, LANES)
    for d in range(2):
        start = product(STEP_CHUNK[d][1], 1 - d, own, other, low).astype(BF16)
        for lane in range(LANES):
            o1s[d, lane] = start[lane * LANE:(lane + 1) * LANE]
            send(o1s.at[d, lane], r1.at[d, lane, 1 - d], rs_s.at[2], rs_r.at[d, lane, 2], ring[d])
    landed(3)
    forward(3)
    ready(2)
    for d in range(2):
        i = STEP_CHUNK[d][1]
        c_ref[i, d] = product(i, d, own, other, low)
    import_group(4)

    def whole_chunk(i):
        own, other, low = operands(0, LANES)
        for half in range(2):
            c_ref[i, half] = product(i, half, own, other, low)

    for lane in range(LANES):
        rows = slice(lane * LANE, (lane + 1) * LANE)
        for d in range(2):
            slot = h0r.at[d, lane]
            arrived(slot, rs_r.at[d, lane, 0])
            h0r[d, lane] = (h0r[d, lane].astype(F32) + c_ref[STEP_CHUNK[d][1], d, rows]).astype(BF16)
            send(slot, r1.at[d, lane, d], rs_s.at[1], rs_r.at[d, lane, 1], ring[d])
    pass_on(3)
    landed(4)
    forward(4)
    loaded(1)
    ready(3)
    for i in range(3, 5):
        whole_chunk(i)

    def add_chunk(buf, d, lane, i):
        for half in range(2):
            rows = slice(lane * LANE, (lane + 1) * LANE)
            buf[d, lane, half] = (buf[d, lane, half].astype(F32) + c_ref[i, half, rows]).astype(BF16)

    for lane in range(LANES):
        for d in range(2):
            for half in range(2):
                msg = 1 if half == d else 2
                arrived(r1.at[d, lane, half], rs_r.at[d, lane, msg])
            add_chunk(r1, d, lane, STEP_CHUNK[d][2])
            send(r1.at[d, lane], r2.at[d, lane], rs_s.at[3], rs_r.at[d, lane, 3], ring[d])
    pass_on(4)
    loaded(2)
    ready(4)
    for i in range(5, 7):
        whole_chunk(i)
    for lane in range(LANES):
        for d in range(2):
            arrived(r2.at[d, lane], rs_r.at[d, lane, 3])
            add_chunk(r2, d, lane, STEP_CHUNK[d][3])
            send(r2.at[d, lane], r3.at[d, lane], rs_s.at[4], rs_r.at[d, lane, 4], ring[d])
    whole_chunk(7)
    for lane in range(LANES):
        rows = slice(lane * LANE, (lane + 1) * LANE)
        for d in range(2):
            arrived(r3.at[d, lane], rs_r.at[d, lane, 4])
        for half in range(2):
            total = c_ref[7, half, rows] + r3[0, lane, half].astype(F32) + r3[1, lane, half].astype(F32)
            out_ref[rows, half * HALF_COLS:(half + 1) * HALF_COLS] = total.astype(BF16)

    for n, buf in enumerate((h0s, h0r, o1s, r1, r2)):
        left(buf, rs_s.at[n])
    part = wo.at[:, 0, 0:64]
    left(part, wx_s.at[0])
    for k in range(1, 4):
        left(part, wy_s.at[k - 1])
    for k in range(4):
        left(part, ws_s.at[k])
    left(up_all.at[0:7], up_s.at[0])
    left(att_o, ax_s.at[0])
    left(dt_o, ax_s.at[0])
    for j in range(2):
        left(kvp.at[j, 0], kv_s.at[j])
    left(kvp.at[:, 0], kv_s.at[4])

    @pl.when(core == 0)
    def _():
        for one in to_sibling:
            one.wait_send()


def body(queries, keys, values, output_matrix, adapter_down_weight, adapter_up_weight):
    vmem = pl.BlockSpec(memory_space=pltpu.VMEM)
    hbm = pl.BlockSpec(memory_space=pl.ANY)
    dma = pltpu.SemaphoreType.DMA
    return pl.pallas_call(
        kernel,
        out_shape=jax.ShapeDtypeStruct((ROWS, COLS), BF16),
        in_specs=[vmem, hbm, hbm, hbm, vmem, vmem],
        out_specs=vmem,
        scratch_shapes=[
            pltpu.VMEM((2, 2, ROWS, HEAD), BF16),
            pltpu.VMEM((2, 2, ROWS, HEAD), BF16),
            pltpu.VMEM((2, 2, ROWS, HEAD), BF16),
            pltpu.VMEM((8, 2, 256, COLS), BF16),
            pltpu.VMEM((16, 2, 256, HALF_COLS), BF16),
            pltpu.VMEM((2, LANES, LANE, 256), BF16),
            pltpu.VMEM((2, LANES, LANE, 256), BF16),
            pltpu.VMEM((2, 3 * RANK, 256), BF16),
            pltpu.VMEM((2, 3 * RANK, 256), BF16),
            pltpu.VMEM((8, RANK, COLS), BF16),
            pltpu.VMEM((LANES, LANE, 3 * RANK), BF16),
            pltpu.VMEM((2, LANES, 2 * LANE, HEAD), F32),
            pltpu.VMEM((2, LANES, 2 * LANE, HEAD), F32),
            pltpu.VMEM((2, LANES, 2 * LANE, HEAD), F32),
            pltpu.VMEM((8, 2, ROWS, HALF_COLS), F32),
            pltpu.VMEM((2, LANES, LANE, HALF_COLS), BF16),
            pltpu.VMEM((2, LANES, LANE, HALF_COLS), BF16),
            pltpu.VMEM((2, LANES, LANE, HALF_COLS), BF16),
            pltpu.VMEM((2, LANES, 2, LANE, HALF_COLS), BF16),
            pltpu.VMEM((2, LANES, 2, LANE, HALF_COLS), BF16),
            pltpu.VMEM((2, LANES, 2, LANE, HALF_COLS), BF16),
            dma((2,)), dma((3,)),
            dma((5,)), dma((6,)),
            dma((1,)), dma((2, 4)),
            dma((1,)), dma((LANES + 2,)),
            dma((1,)), dma((5,)),
            dma((3,)), dma((5, 3)),
            dma((4,)), dma((5, 4)),
            dma((5,)), dma((2, LANES, 5)),
        ],
        compiler_params=pltpu.CompilerParams(
            collective_id=0, has_side_effects=True, vmem_limit_bytes=56 * 2**20
        ),
        cost_estimate=pl.CostEstimate(flops=6 * 10**9, bytes_accessed=12 * 2**20, transcendentals=3 * 10**6),
        name="attend_and_project",
    )(queries, keys, values, output_matrix, jnp.swapaxes(adapter_down_weight, 1, 2), adapter_up_weight)


def solution(mesh):
    return jax.shard_map(
        body,
        mesh=mesh,
        in_specs=(
            P(None, "ctx", "tp"),
            P(None, "ctx", None),
            P(None, "ctx", None),
            P(None, "tp", None),
            P(None, "tp", None),
            P(None, "tp"),
        ),
        out_specs=P("ctx", "tp"),
        check_vma=False,
    )
```

```python
import functools
import math

import jax
import jax.numpy as jnp
from jax import lax
from jax.experimental import pallas as pl
from jax.experimental.pallas import tpu as pltpu
from jax.sharding import PartitionSpec as P

HEAD = 128
ROWS = 512
LANES = 4
LANE = 128
RANK = 16
COLS = 512
HALF_COLS = 256
ADAPTER_SCALE = 2.0
SCORE_SCALE = math.log2(math.e) / math.sqrt(HEAD)
MESH = pl.DeviceIdType.MESH
F32 = jnp.float32
BF16 = jnp.bfloat16

ORDER = (4, 3, 5, 2, 6, 1, 7, 0)
PIECES = ((0, 0), (0, 1), (1, 1), (2, 0), (1, 0), (2, 1)) + tuple((i, half) for i in range(3, 8) for half in range(2))
GROUPS = ((0, 2), (2, 2), (4, 2), (6, 4), (10, 6))
STEP_CHUNK = ((0, 1, 3, 5, 7), (0, 2, 4, 6, 7))


def dot(a, b):
    return jnp.dot(a, b, preferred_element_type=F32)


def dot_nt(a, b):
    return lax.dot_general(a, b, (((1,), (1,)), ((), ())), preferred_element_type=F32)


def kernel(
    q_ref, k_hbm, v_hbm, w_hbm, down_ref, up_ref, out_ref,
    kvo, kvs, kvp, wn, wo, att_o, att_x, dt_o, dt_x, dt_in, up_all, low3,
    m_ref, l_ref, acc_ref, c_ref, h0s, h0r, o1s, r1, r2, r3,
    loc_sem, wn_sem, kv_s, kv_r, up_s, up_r, ax_s, ax_r,
    wx_s, wx_r, wy_s, wy_r, ws_s, ws_r, rs_s, rs_r,
):
    ctx = lax.axis_index("ctx")
    tp = lax.axis_index("tp")
    core = ctx % 2
    y = (ctx // 2) % 4
    x_lo = ctx // 8
    z = tp % 8
    x_hi = tp // 8

    def at_z(k):
        return (ctx, x_hi * 8 + (z + k) % 8)

    def at_y(k):
        return ((x_lo * 4 + (y + k) % 4) * 2 + core, tp)

    sibling = (x_lo * 8 + y * 2 + 1 - core, tp)
    nxt = ((ctx + 2) % 16, tp)
    prv = ((ctx + 14) % 16, tp)
    partner = (ctx, (1 - x_hi) * 8 + z)
    w_partner = ((1 - x_lo) * 8 + y * 2 + core, (1 - x_hi) * 8 + z)

    def copy(src, dst, ss, rs, dev):
        return pltpu.make_async_remote_copy(
            src_ref=src, dst_ref=dst, send_sem=ss, recv_sem=rs, device_id=dev, device_id_type=MESH
        )

    def send(src, dst, ss, rs, dev):
        copy(src, dst, ss, rs, dev).start()

    def arrived(dst, rs):
        copy(dst, dst, kv_s.at[0], rs, sibling).wait_recv()

    def left(src, ss):
        copy(src, src, ss, kv_r.at[0], sibling).wait_send()

    kv_col = pl.ds(pl.multiple_of((tp // 4) * HEAD, HEAD), HEAD)
    load_k = pltpu.make_async_copy(k_hbm.at[:, :, kv_col], kvo.at[0], loc_sem.at[0])
    load_v = pltpu.make_async_copy(v_hbm.at[:, :, kv_col], kvo.at[1], loc_sem.at[1])
    load_k.start()
    load_v.start()

    def col_of(hi, i, half=0, width=COLS):
        first = (hi * 8 + (z + ORDER[i]) % 8) * COLS + half * HALF_COLS
        return pl.ds(pl.multiple_of(first, width), width)

    barrier = pltpu.get_barrier_semaphore()
    friends = [sibling, nxt, prv, partner, w_partner]
    friends += [at_y(k) for k in range(1, 4)] + [at_z(1), at_z(7)]
    for friend in friends:
        pl.semaphore_signal(barrier, inc=1, device_id=friend, device_id_type=MESH)

    for h in range(2):
        dt_o[h] = jnp.concatenate([down_ref[h]] * 3, axis=0)
    up_all[z] = up_ref[...]

    pl.semaphore_wait(barrier, len(friends))

    w_half = y // 2

    def rows_of(who_y, who_core):
        return pl.ds(pl.multiple_of(((who_y % 2) * 2 + who_core) * 64, 64), 64)

    def import_group(g):
        first, count = GROUPS[g]
        for n in range(first, first + count):
            send(
                w_hbm.at[w_half, rows_of(y, core), col_of(1 - x_hi, *PIECES[n], HALF_COLS)],
                wo.at[n, w_half, rows_of(y, core)],
                wx_s.at[0], wx_r.at[g], w_partner,
            )

    def group(g, half, rows):
        first, count = GROUPS[g]
        return wo.at[pl.ds(first, count), half, rows]

    def landed(g):
        arrived(group(g, w_half, rows_of(y, core)), wx_r.at[g])

    def forward(g):
        mine = group(g, w_half, rows_of(y, core))
        for k in range(1, 4):
            send(mine, mine, wy_s.at[k - 1], wy_r.at[g, k - 1], at_y(k))
        send(mine, mine, ws_s.at[0], ws_r.at[g, 0], sibling)

    def pass_on(g):
        for k in range(1, 4):
            other = (y + 4 - k) % 4
            part = group(g, other // 2, rows_of(other, core))
            arrived(part, wy_r.at[g, k - 1])
            send(part, part, ws_s.at[k], ws_r.at[g, k], sibling)

    def ready(g):
        for k in range(4):
            other = (y + 4 - k) % 4
            arrived(group(g, other // 2, rows_of(other, 1 - core)), ws_r.at[g, k])

    def up_step(k):
        for d in range(2):
            if k == 4 and d == 1:
                continue
            slot = up_all.at[(z + (9 - k if d == 0 else k - 1)) % 8]
            if k > 1:
                arrived(slot, up_r.at[d, k - 2])
            send(slot, slot, up_s.at[0], up_r.at[d, k - 1], ring[d])

    ring = (at_z(1), at_z(7))
    small = y % 2
    large = 1 - small
    kv = (k_hbm, v_hbm)
    for j in range(2):
        send(kv[j].at[small, :, kv_col], kvp.at[j, core], kv_s.at[j], kv_r.at[j], nxt)
    for g in range(3):
        import_group(g)
    to_sibling = [
        copy(kv[j].at[:, :, kv_col], kvs.at[j], kv_s.at[2 + j], kv_r.at[2 + j], sibling)
        for j in range(2)
    ]

    @pl.when(core == 0)
    def _():
        for one in to_sibling:
            one.start()

    send(down_ref, dt_in, ax_s.at[0], ax_r.at[LANES], partner)

    up_step(1)

    load_w = [
        pltpu.make_async_copy(w_hbm.at[:, :, col_of(x_hi, i)], wn.at[i], wn_sem.at[i // 3]) for i in range(8)
    ]
    for one in load_w:
        one.start()

    def loaded(n):
        part = wn.at[3 * n:min(3 * n + 3, 8)]
        pltpu.make_async_copy(part, part, wn_sem.at[n]).wait()

    load_k.wait()
    load_v.wait()

    def queries_of(h, lane):
        rows = pl.ds(pl.multiple_of(lane * LANE, LANE), LANE)
        return jnp.concatenate([q_ref[h, rows, 0:HEAD], q_ref[h, rows, HEAD:2 * HEAD]], axis=0)

    def own_keys(t):
        h = (small + t) % 2
        for lane in range(LANES):
            q = queries_of(h, lane)
            edge = lane * LANE
            s1 = dot_nt(q, kvo[0, h, edge:edge + LANE, :]) * SCORE_SCALE
            row = lax.broadcasted_iota(jnp.int32, s1.shape, 0) % LANE
            col = lax.broadcasted_iota(jnp.int32, s1.shape, 1)
            s1 = jnp.where(col <= row, s1, -jnp.inf)
            m = jnp.max(s1, axis=1, keepdims=True)
            if lane:
                s0 = dot_nt(q, kvo[0, h, 0:edge, :]) * SCORE_SCALE
                m = jnp.maximum(m, jnp.max(s0, axis=1, keepdims=True))
            p1 = jnp.exp2(s1 - m)
            total = jnp.sum(p1, axis=1, keepdims=True)
            acc = dot(p1.astype(BF16), kvo[1, h, edge:edge + LANE, :])
            if lane:
                p0 = jnp.exp2(s0 - m)
                total = total + jnp.sum(p0, axis=1, keepdims=True)
                acc = acc + dot(p0.astype(BF16), kvo[1, h, 0:edge, :])
            m_ref[t, lane] = jnp.broadcast_to(m, (2 * LANE, HEAD))
            l_ref[t, lane] = jnp.broadcast_to(total, (2 * LANE, HEAD))
            acc_ref[t, lane] = acc

    def more_keys(t, h, lane, keys, vals):
        s = dot_nt(queries_of(h, lane), keys) * SCORE_SCALE
        m_old = m_ref[t, lane][:, 0:1]
        m = jnp.maximum(m_old, jnp.max(s, axis=1, keepdims=True))
        scale = jnp.exp2(m_old - m)
        p = jnp.exp2(s - m)
        total = l_ref[t, lane][:, 0:1] * scale + jnp.sum(p, axis=1, keepdims=True)
        acc = acc_ref[t, lane] * scale + dot(p.astype(BF16), vals)
        return m, total, acc

    def keep(t, lane, state):
        m, total, acc = state
        m_ref[t, lane] = jnp.broadcast_to(m, (2 * LANE, HEAD))
        l_ref[t, lane] = jnp.broadcast_to(total, (2 * LANE, HEAD))
        acc_ref[t, lane] = acc

    def finish(h, lane, total, acc):
        att = (acc / total).astype(BF16)
        att_o[h, lane, :, 0:HEAD] = att[0:LANE]
        att_o[h, lane, :, HEAD:2 * HEAD] = att[LANE:2 * LANE]

    def sibling_keys(t):
        h = (small + t) % 2

        def one_lane(lane, carry):
            keep(t, lane, more_keys(t, h, lane, kvs[0, h], kvs[1, h]))
            return carry

        lax.fori_loop(0, LANES, one_lane, 0)

    own_keys(0)

    @pl.when(core == 1)
    def _():
        for j in range(2):
            to_sibling[j].wait_recv()
        sibling_keys(0)

    for lane in range(LANES):
        finish(small, lane, l_ref[0, lane][:, 0:1], acc_ref[0, lane])
    landed(0)
    landed(1)
    forward(0)
    forward(1)
    landed(2)
    send(att_o.at[small], att_x.at[small], ax_s.at[0], ax_r.at[LANES + 1], partner)
    up_step(2)
    own_keys(1)

    @pl.when(core == 1)
    def _():
        sibling_keys(1)

    up_step(3)
    for j in range(2):
        arrived(kvp.at[j, core], kv_r.at[j])
        send(kvp.at[j, core], kvp.at[j, core], kv_s.at[4], kv_r.at[4 + j], sibling)

    forward(2)

    def pair_keys(lane, carry):
        keep(1, lane, more_keys(1, large, lane, kvp[0, core], kvp[1, core]))
        return carry

    lax.fori_loop(0, LANES, pair_keys, 0)
    up_step(4)
    pass_on(0)
    for j in range(2):
        arrived(kvp.at[j, 1 - core], kv_r.at[4 + j])
    for lane in range(LANES):
        _, total, acc = more_keys(1, large, lane, kvp[0, 1 - core], kvp[1, 1 - core])
        finish(large, lane, total, acc)
        send(att_o.at[large, lane], att_x.at[large, lane], ax_s.at[0], ax_r.at[lane], partner)
    pass_on(1)

    arrived(dt_in, ax_r.at[LANES])
    for h in range(2):
        dt_x[h] = jnp.concatenate([dt_in[h]] * 3, axis=0)
    arrived(att_x.at[small], ax_r.at[LANES + 1])
    arrived(up_all.at[(z + 4) % 8], up_r.at[0, 3])
    arrived(up_all.at[(z + 3) % 8], up_r.at[1, 2])
    loaded(0)
    ready(0)

    def own_product(i, half, own, low):
        cols = slice(half * HALF_COLS, (half + 1) * HALF_COLS)
        up = up_all[(z + ORDER[i]) % 8, :, cols]
        out = dot(low, jnp.concatenate([up, up, up], axis=0))
        for h in range(2):
            out = out + dot(own[h], wn[i, h, :, cols])
        return out

    def partner_product(i, half, other):
        n = PIECES.index((i, half))
        return dot(other[0], wo[n, 0]) + dot(other[1], wo[n, 1])

    def product(i, half, own, other, low):
        return own_product(i, half, own, low) + partner_product(i, half, other)

    def operands(first, count):
        rows = slice(first, first + count)
        own = [att_o[h, rows].reshape(count * LANE, 2 * HEAD) for h in range(2)]
        other = [att_x[h, rows].reshape(count * LANE, 2 * HEAD) for h in range(2)]
        return own, other, low3[rows].reshape(count * LANE, 3 * RANK)

    for lane in range(LANES):
        arrived(att_x.at[large, lane], ax_r.at[lane])
        low = jnp.zeros((LANE, 3 * RANK), F32)
        for h in range(2):
            low = low + dot_nt(att_o[h, lane], dt_o[h]) + dot_nt(att_x[h, lane], dt_x[h])
        low = low * ADAPTER_SCALE
        top = low.astype(BF16).astype(F32)
        rest = low - top
        mid = rest.astype(BF16).astype(F32)
        third = lax.broadcasted_iota(jnp.int32, low.shape, 1) // RANK
        low3[lane] = jnp.where(third == 0, top, jnp.where(third == 1, mid, rest - mid)).astype(BF16)
        own, other, low = operands(lane, 1)
        for d in range(2):
            h0s[d, lane] = product(0, d, own, other, low).astype(BF16)
            send(h0s.at[d, lane], h0r.at[d, lane], rs_s.at[0], rs_r.at[d, lane, 0], ring[d])
        if lane == 0:
            import_group(3)
        if lane == 2:
            pass_on(2)
    ready(1)
    own, other, low = operands(0, LANES)
    for d in range(2):
        start = product(STEP_CHUNK[d][1], 1 - d, own, other, low).astype(BF16)
        for lane in range(LANES):
            o1s[d, lane] = start[lane * LANE:(lane + 1) * LANE]
            send(o1s.at[d, lane], r1.at[d, lane, 1 - d], rs_s.at[2], rs_r.at[d, lane, 2], ring[d])
    landed(3)
    forward(3)
    for d in range(2):
        i = STEP_CHUNK[d][1]
        c_ref[i, d] = own_product(i, d, own, low)
    ready(2)
    for d in range(2):
        i = STEP_CHUNK[d][1]
        c_ref[i, d] += partner_product(i, d, other)
    import_group(4)

    def own_chunk(i):
        own, _, low = operands(0, LANES)
        for half in range(2):
            c_ref[i, half] = own_product(i, half, own, low)

    def partner_chunk(i):
        _, other, _ = operands(0, LANES)
        for half in range(2):
            c_ref[i, half] += partner_product(i, half, other)

    for lane in range(LANES):
        rows = slice(lane * LANE, (lane + 1) * LANE)
        for d in range(2):
            slot = h0r.at[d, lane]
            arrived(slot, rs_r.at[d, lane, 0])
            h0r[d, lane] = (h0r[d, lane].astype(F32) + c_ref[STEP_CHUNK[d][1], d, rows]).astype(BF16)
            send(slot, r1.at[d, lane, d], rs_s.at[1], rs_r.at[d, lane, 1], ring[d])
    pass_on(3)
    landed(4)
    forward(4)
    loaded(1)
    for i in range(3, 5):
        own_chunk(i)
    ready(3)
    for i in range(3, 5):
        partner_chunk(i)

    def add_chunk(buf, d, lane, i):
        for half in range(2):
            rows = slice(lane * LANE, (lane + 1) * LANE)
            buf[d, lane, half] = (buf[d, lane, half].astype(F32) + c_ref[i, half, rows]).astype(BF16)

    for lane in range(LANES):
        for d in range(2):
            for half in range(2):
                msg = 1 if half == d else 2
                arrived(r1.at[d, lane, half], rs_r.at[d, lane, msg])
            add_chunk(r1, d, lane, STEP_CHUNK[d][2])
            send(r1.at[d, lane], r2.at[d, lane], rs_s.at[3], rs_r.at[d, lane, 3], ring[d])
    pass_on(4)
    loaded(2)
    for i in range(5, 7):
        own_chunk(i)
    ready(4)
    for i in range(5, 7):
        partner_chunk(i)
    for lane in range(LANES):
        for d in range(2):
            arrived(r2.at[d, lane], rs_r.at[d, lane, 3])
            add_chunk(r2, d, lane, STEP_CHUNK[d][3])
            send(r2.at[d, lane], r3.at[d, lane], rs_s.at[4], rs_r.at[d, lane, 4], ring[d])
    own_chunk(7)
    partner_chunk(7)
    for lane in range(LANES):
        rows = slice(lane * LANE, (lane + 1) * LANE)
        for d in range(2):
            arrived(r3.at[d, lane], rs_r.at[d, lane, 4])
        for half in range(2):
            total = c_ref[7, half, rows] + r3[0, lane, half].astype(F32) + r3[1, lane, half].astype(F32)
            out_ref[rows, half * HALF_COLS:(half + 1) * HALF_COLS] = total.astype(BF16)

    for n, buf in enumerate((h0s, h0r, o1s, r1, r2)):
        left(buf, rs_s.at[n])
    part = wo.at[:, 0, 0:64]
    left(part, wx_s.at[0])
    for k in range(1, 4):
        left(part, wy_s.at[k - 1])
    for k in range(4):
        left(part, ws_s.at[k])
    left(up_all.at[0:7], up_s.at[0])
    left(att_o, ax_s.at[0])
    left(dt_in, ax_s.at[0])
    for j in range(2):
        left(kvp.at[j, 0], kv_s.at[j])
    left(kvp.at[:, 0], kv_s.at[4])

    @pl.when(core == 0)
    def _():
        for one in to_sibling:
            one.wait_send()


def body(queries, keys, values, output_matrix, adapter_down_weight, adapter_up_weight):
    vmem = pl.BlockSpec(memory_space=pltpu.VMEM)
    hbm = pl.BlockSpec(memory_space=pl.ANY)
    dma = pltpu.SemaphoreType.DMA
    return pl.pallas_call(
        kernel,
        out_shape=jax.ShapeDtypeStruct((ROWS, COLS), BF16),
        in_specs=[vmem, hbm, hbm, hbm, vmem, vmem],
        out_specs=vmem,
        scratch_shapes=[
            pltpu.VMEM((2, 2, ROWS, HEAD), BF16),
            pltpu.VMEM((2, 2, ROWS, HEAD), BF16),
            pltpu.VMEM((2, 2, ROWS, HEAD), BF16),
            pltpu.VMEM((8, 2, 256, COLS), BF16),
            pltpu.VMEM((16, 2, 256, HALF_COLS), BF16),
            pltpu.VMEM((2, LANES, LANE, 256), BF16),
            pltpu.VMEM((2, LANES, LANE, 256), BF16),
            pltpu.VMEM((2, 3 * RANK, 256), BF16),
            pltpu.VMEM((2, 3 * RANK, 256), BF16),
            pltpu.VMEM((2, RANK, 256), BF16),
            pltpu.VMEM((8, RANK, COLS), BF16),
            pltpu.VMEM((LANES, LANE, 3 * RANK), BF16),
            pltpu.VMEM((2, LANES, 2 * LANE, HEAD), F32),
            pltpu.VMEM((2, LANES, 2 * LANE, HEAD), F32),
            pltpu.VMEM((2, LANES, 2 * LANE, HEAD), F32),
            pltpu.VMEM((8, 2, ROWS, HALF_COLS), F32),
            pltpu.VMEM((2, LANES, LANE, HALF_COLS), BF16),
            pltpu.VMEM((2, LANES, LANE, HALF_COLS), BF16),
            pltpu.VMEM((2, LANES, LANE, HALF_COLS), BF16),
            pltpu.VMEM((2, LANES, 2, LANE, HALF_COLS), BF16),
            pltpu.VMEM((2, LANES, 2, LANE, HALF_COLS), BF16),
            pltpu.VMEM((2, LANES, 2, LANE, HALF_COLS), BF16),
            dma((2,)), dma((3,)),
            dma((5,)), dma((6,)),
            dma((1,)), dma((2, 4)),
            dma((1,)), dma((LANES + 2,)),
            dma((1,)), dma((5,)),
            dma((3,)), dma((5, 3)),
            dma((4,)), dma((5, 4)),
            dma((5,)), dma((2, LANES, 5)),
        ],
        compiler_params=pltpu.CompilerParams(
            collective_id=0, has_side_effects=True, vmem_limit_bytes=56 * 2**20
        ),
        cost_estimate=pl.CostEstimate(flops=6 * 10**9, bytes_accessed=12 * 2**20, transcendentals=3 * 10**6),
        name="attend_and_project",
    )(queries, keys, values, output_matrix, jnp.swapaxes(adapter_down_weight, 1, 2), adapter_up_weight)


def solution(mesh):
    return jax.shard_map(
        body,
        mesh=mesh,
        in_specs=(
            P(None, "ctx", "tp"),
            P(None, "ctx", None),
            P(None, "ctx", None),
            P(None, "tp", None),
            P(None, "tp", None),
            P(None, "tp"),
        ),
        out_specs=P("ctx", "tp"),
        check_vma=False,
    )
```

```python
import functools
import math

import jax
import jax.numpy as jnp
from jax import lax
from jax.experimental import pallas as pl
from jax.experimental.pallas import tpu as pltpu
from jax.sharding import PartitionSpec as P

HEAD = 128
ROWS = 512
LANES = 4
LANE = 128
RANK = 16
COLS = 512
HALF_COLS = 256
ADAPTER_SCALE = 2.0
SCORE_SCALE = math.log2(math.e) / math.sqrt(HEAD)
MESH = pl.DeviceIdType.MESH
F32 = jnp.float32
BF16 = jnp.bfloat16

ORDER = (4, 3, 5, 2, 6, 1, 7, 0)
PIECES = ((0, 0), (0, 1), (1, 1), (2, 0), (1, 0), (2, 1)) + tuple((i, half) for i in range(3, 8) for half in range(2))
GROUPS = ((0, 2), (2, 2), (4, 2), (6, 4), (10, 6))
STEP_CHUNK = ((0, 1, 3, 5, 7), (0, 2, 4, 6, 7))


def dot(a, b):
    return jnp.dot(a, b, preferred_element_type=F32)


def dot_nt(a, b):
    return lax.dot_general(a, b, (((1,), (1,)), ((), ())), preferred_element_type=F32)


def kernel(
    q_ref, k_hbm, v_hbm, w_hbm, down_ref, up_ref, out_ref,
    kvo, kvs, kvp, wn, wo, att_o, att_x, dt_o, dt_x, dt_in, up_all, low3,
    m_ref, l_ref, acc_ref, c_ref, h0s, h0r, o1s, r1, r2, r3,
    loc_sem, wn_sem, kv_s, kv_r, up_s, up_r, ax_s, ax_r,
    wx_s, wx_r, wy_s, wy_r, ws_s, ws_r, rs_s, rs_r,
):
    ctx = lax.axis_index("ctx")
    tp = lax.axis_index("tp")
    core = ctx % 2
    y = (ctx // 2) % 4
    x_lo = ctx // 8
    z = tp % 8
    x_hi = tp // 8

    def at_z(k):
        return (ctx, x_hi * 8 + (z + k) % 8)

    def at_y(k):
        return ((x_lo * 4 + (y + k) % 4) * 2 + core, tp)

    sibling = (x_lo * 8 + y * 2 + 1 - core, tp)
    nxt = ((ctx + 2) % 16, tp)
    prv = ((ctx + 14) % 16, tp)
    partner = (ctx, (1 - x_hi) * 8 + z)
    w_partner = ((1 - x_lo) * 8 + y * 2 + core, (1 - x_hi) * 8 + z)

    def copy(src, dst, ss, rs, dev):
        return pltpu.make_async_remote_copy(
            src_ref=src, dst_ref=dst, send_sem=ss, recv_sem=rs, device_id=dev, device_id_type=MESH
        )

    def send(src, dst, ss, rs, dev):
        copy(src, dst, ss, rs, dev).start()

    def arrived(dst, rs):
        copy(dst, dst, kv_s.at[0], rs, sibling).wait_recv()

    def left(src, ss):
        copy(src, src, ss, kv_r.at[0], sibling).wait_send()

    kv_col = pl.ds(pl.multiple_of((tp // 4) * HEAD, HEAD), HEAD)
    load_k = pltpu.make_async_copy(k_hbm.at[:, :, kv_col], kvo.at[0], loc_sem.at[0])
    load_v = pltpu.make_async_copy(v_hbm.at[:, :, kv_col], kvo.at[1], loc_sem.at[1])
    load_k.start()
    load_v.start()

    def col_of(hi, i, half=0, width=COLS):
        first = (hi * 8 + (z + ORDER[i]) % 8) * COLS + half * HALF_COLS
        return pl.ds(pl.multiple_of(first, width), width)

    barrier = pltpu.get_barrier_semaphore()
    friends = [sibling, nxt, prv, partner, w_partner]
    friends += [at_y(k) for k in range(1, 4)] + [at_z(1), at_z(7)]
    for friend in friends:
        pl.semaphore_signal(barrier, inc=1, device_id=friend, device_id_type=MESH)

    for h in range(2):
        dt_o[h] = jnp.concatenate([down_ref[h]] * 3, axis=0)
    up_all[z] = up_ref[...]

    pl.semaphore_wait(barrier, len(friends))

    w_half = y // 2

    def rows_of(who_y, who_core):
        return pl.ds(pl.multiple_of(((who_y % 2) * 2 + who_core) * 64, 64), 64)

    def import_group(g):
        first, count = GROUPS[g]
        for n in range(first, first + count):
            send(
                w_hbm.at[w_half, rows_of(y, core), col_of(1 - x_hi, *PIECES[n], HALF_COLS)],
                wo.at[n, w_half, rows_of(y, core)],
                wx_s.at[0], wx_r.at[g], w_partner,
            )

    def group(g, half, rows):
        first, count = GROUPS[g]
        return wo.at[pl.ds(first, count), half, rows]

    def landed(g):
        arrived(group(g, w_half, rows_of(y, core)), wx_r.at[g])

    def forward(g):
        mine = group(g, w_half, rows_of(y, core))
        for k in range(1, 4):
            send(mine, mine, wy_s.at[k - 1], wy_r.at[g, k - 1], at_y(k))
        send(mine, mine, ws_s.at[0], ws_r.at[g, 0], sibling)

    def pass_on(g):
        for k in range(1, 4):
            other = (y + 4 - k) % 4
            part = group(g, other // 2, rows_of(other, core))
            arrived(part, wy_r.at[g, k - 1])
            send(part, part, ws_s.at[k], ws_r.at[g, k], sibling)

    def ready(g):
        for k in range(4):
            other = (y + 4 - k) % 4
            arrived(group(g, other // 2, rows_of(other, 1 - core)), ws_r.at[g, k])

    def up_step(k):
        for d in range(2):
            if k == 4 and d == 1:
                continue
            slot = up_all.at[(z + (9 - k if d == 0 else k - 1)) % 8]
            if k > 1:
                arrived(slot, up_r.at[d, k - 2])
            send(slot, slot, up_s.at[0], up_r.at[d, k - 1], ring[d])

    ring = (at_z(1), at_z(7))
    small = y % 2
    large = 1 - small
    kv = (k_hbm, v_hbm)
    for j in range(2):
        send(kv[j].at[small, :, kv_col], kvp.at[j, core], kv_s.at[j], kv_r.at[j], nxt)
    for g in range(3):
        import_group(g)
    to_sibling = [
        copy(kv[j].at[:, :, kv_col], kvs.at[j], kv_s.at[2 + j], kv_r.at[2 + j], sibling)
        for j in range(2)
    ]

    @pl.when(core == 0)
    def _():
        for one in to_sibling:
            one.start()

    send(down_ref, dt_in, ax_s.at[0], ax_r.at[LANES], partner)

    up_step(1)

    load_w = [
        pltpu.make_async_copy(w_hbm.at[:, :, col_of(x_hi, i)], wn.at[i], wn_sem.at[i // 3]) for i in range(8)
    ]
    for one in load_w:
        one.start()

    def loaded(n):
        part = wn.at[3 * n:min(3 * n + 3, 8)]
        pltpu.make_async_copy(part, part, wn_sem.at[n]).wait()

    load_k.wait()
    load_v.wait()

    def queries_of(h, lane):
        rows = pl.ds(pl.multiple_of(lane * LANE, LANE), LANE)
        return jnp.concatenate([q_ref[h, rows, 0:HEAD], q_ref[h, rows, HEAD:2 * HEAD]], axis=0)

    def own_keys(t):
        h = (small + t) % 2
        for lane in range(LANES):
            q = queries_of(h, lane)
            edge = lane * LANE
            s1 = dot_nt(q, kvo[0, h, edge:edge + LANE, :]) * SCORE_SCALE
            row = lax.broadcasted_iota(jnp.int32, s1.shape, 0) % LANE
            col = lax.broadcasted_iota(jnp.int32, s1.shape, 1)
            s1 = jnp.where(col <= row, s1, -jnp.inf)
            m = jnp.max(s1, axis=1, keepdims=True)
            if lane:
                s0 = dot_nt(q, kvo[0, h, 0:edge, :]) * SCORE_SCALE
                m = jnp.maximum(m, jnp.max(s0, axis=1, keepdims=True))
            p1 = jnp.exp2(s1 - m)
            total = jnp.sum(p1, axis=1, keepdims=True)
            acc = dot(p1.astype(BF16), kvo[1, h, edge:edge + LANE, :])
            if lane:
                p0 = jnp.exp2(s0 - m)
                total = total + jnp.sum(p0, axis=1, keepdims=True)
                acc = acc + dot(p0.astype(BF16), kvo[1, h, 0:edge, :])
            m_ref[t, lane] = jnp.broadcast_to(m, (2 * LANE, HEAD))
            l_ref[t, lane] = jnp.broadcast_to(total, (2 * LANE, HEAD))
            acc_ref[t, lane] = acc

    def more_keys(t, h, lane, keys, vals):
        s = dot_nt(queries_of(h, lane), keys) * SCORE_SCALE
        m_old = m_ref[t, lane][:, 0:1]
        m = jnp.maximum(m_old, jnp.max(s, axis=1, keepdims=True))
        scale = jnp.exp2(m_old - m)
        p = jnp.exp2(s - m)
        total = l_ref[t, lane][:, 0:1] * scale + jnp.sum(p, axis=1, keepdims=True)
        acc = acc_ref[t, lane] * scale + dot(p.astype(BF16), vals)
        return m, total, acc

    def keep(t, lane, state):
        m, total, acc = state
        m_ref[t, lane] = jnp.broadcast_to(m, (2 * LANE, HEAD))
        l_ref[t, lane] = jnp.broadcast_to(total, (2 * LANE, HEAD))
        acc_ref[t, lane] = acc

    def finish(h, lane, total, acc):
        att = (acc / total).astype(BF16)
        att_o[h, lane, :, 0:HEAD] = att[0:LANE]
        att_o[h, lane, :, HEAD:2 * HEAD] = att[LANE:2 * LANE]

    def sibling_keys(t):
        h = (small + t) % 2

        def one_lane(lane, carry):
            keep(t, lane, more_keys(t, h, lane, kvs[0, h], kvs[1, h]))
            return carry

        lax.fori_loop(0, LANES, one_lane, 0)

    own_keys(0)

    @pl.when(core == 1)
    def _():
        for j in range(2):
            to_sibling[j].wait_recv()
        sibling_keys(0)

    for lane in range(LANES):
        finish(small, lane, l_ref[0, lane][:, 0:1], acc_ref[0, lane])
    landed(0)
    landed(1)
    forward(0)
    forward(1)
    landed(2)
    send(att_o.at[small], att_x.at[small], ax_s.at[0], ax_r.at[LANES + 1], partner)
    up_step(2)
    own_keys(1)

    @pl.when(core == 1)
    def _():
        sibling_keys(1)

    up_step(3)
    for j in range(2):
        arrived(kvp.at[j, core], kv_r.at[j])
        send(kvp.at[j, core], kvp.at[j, core], kv_s.at[4], kv_r.at[4 + j], sibling)

    forward(2)

    def pair_keys(lane, carry):
        keep(1, lane, more_keys(1, large, lane, kvp[0, core], kvp[1, core]))
        return carry

    lax.fori_loop(0, LANES, pair_keys, 0)
    up_step(4)
    pass_on(0)
    for j in range(2):
        arrived(kvp.at[j, 1 - core], kv_r.at[4 + j])
    for lane in range(LANES):
        _, total, acc = more_keys(1, large, lane, kvp[0, 1 - core], kvp[1, 1 - core])
        finish(large, lane, total, acc)
        send(att_o.at[large, lane], att_x.at[large, lane], ax_s.at[0], ax_r.at[lane], partner)
    pass_on(1)


    def low_product(i, half, low):
        up = up_all[(z + ORDER[i]) % 8, :, half * HALF_COLS:(half + 1) * HALF_COLS]
        return dot(low, jnp.concatenate([up, up, up], axis=0))

    def flat_product(i, half, own):
        cols = slice(half * HALF_COLS, (half + 1) * HALF_COLS)
        return dot(own[0], wn[i, 0, :, cols]) + dot(own[1], wn[i, 1, :, cols])

    def own_product(i, half, own, low):
        return low_product(i, half, low) + flat_product(i, half, own)

    def partner_product(i, half, other):
        n = PIECES.index((i, half))
        return dot(other[0], wo[n, 0]) + dot(other[1], wo[n, 1])

    def product(i, half, own, other, low):
        return own_product(i, half, own, low) + partner_product(i, half, other)

    def operands(first, count):
        rows = slice(first, first + count)
        own = [att_o[h, rows].reshape(count * LANE, 2 * HEAD) for h in range(2)]
        other = [att_x[h, rows].reshape(count * LANE, 2 * HEAD) for h in range(2)]
        return own, other, low3[rows].reshape(count * LANE, 3 * RANK)

    loaded(0)
    own = [att_o[h].reshape(LANES * LANE, 2 * HEAD) for h in range(2)]
    for d in range(2):
        c_ref[0, d] = flat_product(0, d, own)
    arrived(dt_in, ax_r.at[LANES])
    for h in range(2):
        dt_x[h] = jnp.concatenate([dt_in[h]] * 3, axis=0)
    arrived(att_x.at[small], ax_r.at[LANES + 1])
    arrived(up_all.at[(z + 4) % 8], up_r.at[0, 3])
    arrived(up_all.at[(z + 3) % 8], up_r.at[1, 2])
    ready(0)
    for lane in range(LANES):
        arrived(att_x.at[large, lane], ax_r.at[lane])
        low = jnp.zeros((LANE, 3 * RANK), F32)
        for h in range(2):
            low = low + dot_nt(att_o[h, lane], dt_o[h]) + dot_nt(att_x[h, lane], dt_x[h])
        low = low * ADAPTER_SCALE
        top = low.astype(BF16).astype(F32)
        rest = low - top
        mid = rest.astype(BF16).astype(F32)
        third = lax.broadcasted_iota(jnp.int32, low.shape, 1) // RANK
        low3[lane] = jnp.where(third == 0, top, jnp.where(third == 1, mid, rest - mid)).astype(BF16)
        _, other, low = operands(lane, 1)
        rows = slice(lane * LANE, (lane + 1) * LANE)
        for d in range(2):
            part = c_ref[0, d, rows] + low_product(0, d, low) + partner_product(0, d, other)
            h0s[d, lane] = part.astype(BF16)
            send(h0s.at[d, lane], h0r.at[d, lane], rs_s.at[0], rs_r.at[d, lane, 0], ring[d])
        if lane == 0:
            import_group(3)
        if lane == 2:
            pass_on(2)
    ready(1)
    own, other, low = operands(0, LANES)
    for d in range(2):
        start = product(STEP_CHUNK[d][1], 1 - d, own, other, low).astype(BF16)
        for lane in range(LANES):
            o1s[d, lane] = start[lane * LANE:(lane + 1) * LANE]
            send(o1s.at[d, lane], r1.at[d, lane, 1 - d], rs_s.at[2], rs_r.at[d, lane, 2], ring[d])
    landed(3)
    forward(3)
    for d in range(2):
        i = STEP_CHUNK[d][1]
        c_ref[i, d] = own_product(i, d, own, low)
    ready(2)
    for d in range(2):
        i = STEP_CHUNK[d][1]
        c_ref[i, d] += partner_product(i, d, other)
    import_group(4)

    def own_chunk(i):
        own, _, low = operands(0, LANES)
        for half in range(2):
            c_ref[i, half] = own_product(i, half, own, low)

    def partner_chunk(i):
        _, other, _ = operands(0, LANES)
        for half in range(2):
            c_ref[i, half] += partner_product(i, half, other)

    for lane in range(LANES):
        rows = slice(lane * LANE, (lane + 1) * LANE)
        for d in range(2):
            slot = h0r.at[d, lane]
            arrived(slot, rs_r.at[d, lane, 0])
            h0r[d, lane] = (h0r[d, lane].astype(F32) + c_ref[STEP_CHUNK[d][1], d, rows]).astype(BF16)
            send(slot, r1.at[d, lane, d], rs_s.at[1], rs_r.at[d, lane, 1], ring[d])
    pass_on(3)
    landed(4)
    forward(4)
    loaded(1)
    for i in range(3, 5):
        own_chunk(i)
    ready(3)
    for i in range(3, 5):
        partner_chunk(i)

    def add_chunk(buf, d, lane, i):
        for half in range(2):
            rows = slice(lane * LANE, (lane + 1) * LANE)
            buf[d, lane, half] = (buf[d, lane, half].astype(F32) + c_ref[i, half, rows]).astype(BF16)

    for lane in range(LANES):
        for d in range(2):
            for half in range(2):
                msg = 1 if half == d else 2
                arrived(r1.at[d, lane, half], rs_r.at[d, lane, msg])
            add_chunk(r1, d, lane, STEP_CHUNK[d][2])
            send(r1.at[d, lane], r2.at[d, lane], rs_s.at[3], rs_r.at[d, lane, 3], ring[d])
    pass_on(4)
    loaded(2)
    for i in range(5, 7):
        own_chunk(i)
    ready(4)
    for i in range(5, 7):
        partner_chunk(i)
    for lane in range(LANES):
        for d in range(2):
            arrived(r2.at[d, lane], rs_r.at[d, lane, 3])
            add_chunk(r2, d, lane, STEP_CHUNK[d][3])
            send(r2.at[d, lane], r3.at[d, lane], rs_s.at[4], rs_r.at[d, lane, 4], ring[d])
    own_chunk(7)
    partner_chunk(7)
    for lane in range(LANES):
        rows = slice(lane * LANE, (lane + 1) * LANE)
        for d in range(2):
            arrived(r3.at[d, lane], rs_r.at[d, lane, 4])
        for half in range(2):
            total = c_ref[7, half, rows] + r3[0, lane, half].astype(F32) + r3[1, lane, half].astype(F32)
            out_ref[rows, half * HALF_COLS:(half + 1) * HALF_COLS] = total.astype(BF16)

    for n, buf in enumerate((h0s, h0r, o1s, r1, r2)):
        left(buf, rs_s.at[n])
    part = wo.at[:, 0, 0:64]
    left(part, wx_s.at[0])
    for k in range(1, 4):
        left(part, wy_s.at[k - 1])
    for k in range(4):
        left(part, ws_s.at[k])
    left(up_all.at[0:7], up_s.at[0])
    left(att_o, ax_s.at[0])
    left(dt_in, ax_s.at[0])
    for j in range(2):
        left(kvp.at[j, 0], kv_s.at[j])
    left(kvp.at[:, 0], kv_s.at[4])

    @pl.when(core == 0)
    def _():
        for one in to_sibling:
            one.wait_send()


def body(queries, keys, values, output_matrix, adapter_down_weight, adapter_up_weight):
    vmem = pl.BlockSpec(memory_space=pltpu.VMEM)
    hbm = pl.BlockSpec(memory_space=pl.ANY)
    dma = pltpu.SemaphoreType.DMA
    return pl.pallas_call(
        kernel,
        out_shape=jax.ShapeDtypeStruct((ROWS, COLS), BF16),
        in_specs=[vmem, hbm, hbm, hbm, vmem, vmem],
        out_specs=vmem,
        scratch_shapes=[
            pltpu.VMEM((2, 2, ROWS, HEAD), BF16),
            pltpu.VMEM((2, 2, ROWS, HEAD), BF16),
            pltpu.VMEM((2, 2, ROWS, HEAD), BF16),
            pltpu.VMEM((8, 2, 256, COLS), BF16),
            pltpu.VMEM((16, 2, 256, HALF_COLS), BF16),
            pltpu.VMEM((2, LANES, LANE, 256), BF16),
            pltpu.VMEM((2, LANES, LANE, 256), BF16),
            pltpu.VMEM((2, 3 * RANK, 256), BF16),
            pltpu.VMEM((2, 3 * RANK, 256), BF16),
            pltpu.VMEM((2, RANK, 256), BF16),
            pltpu.VMEM((8, RANK, COLS), BF16),
            pltpu.VMEM((LANES, LANE, 3 * RANK), BF16),
            pltpu.VMEM((2, LANES, 2 * LANE, HEAD), F32),
            pltpu.VMEM((2, LANES, 2 * LANE, HEAD), F32),
            pltpu.VMEM((2, LANES, 2 * LANE, HEAD), F32),
            pltpu.VMEM((8, 2, ROWS, HALF_COLS), F32),
            pltpu.VMEM((2, LANES, LANE, HALF_COLS), BF16),
            pltpu.VMEM((2, LANES, LANE, HALF_COLS), BF16),
            pltpu.VMEM((2, LANES, LANE, HALF_COLS), BF16),
            pltpu.VMEM((2, LANES, 2, LANE, HALF_COLS), BF16),
            pltpu.VMEM((2, LANES, 2, LANE, HALF_COLS), BF16),
            pltpu.VMEM((2, LANES, 2, LANE, HALF_COLS), BF16),
            dma((2,)), dma((3,)),
            dma((5,)), dma((6,)),
            dma((1,)), dma((2, 4)),
            dma((1,)), dma((LANES + 2,)),
            dma((1,)), dma((5,)),
            dma((3,)), dma((5, 3)),
            dma((4,)), dma((5, 4)),
            dma((5,)), dma((2, LANES, 5)),
        ],
        compiler_params=pltpu.CompilerParams(
            collective_id=0, has_side_effects=True, vmem_limit_bytes=56 * 2**20
        ),
        cost_estimate=pl.CostEstimate(flops=6 * 10**9, bytes_accessed=12 * 2**20, transcendentals=3 * 10**6),
        name="attend_and_project",
    )(queries, keys, values, output_matrix, jnp.swapaxes(adapter_down_weight, 1, 2), adapter_up_weight)


def solution(mesh):
    return jax.shard_map(
        body,
        mesh=mesh,
        in_specs=(
            P(None, "ctx", "tp"),
            P(None, "ctx", None),
            P(None, "ctx", None),
            P(None, "tp", None),
            P(None, "tp", None),
            P(None, "tp"),
        ),
        out_specs=P("ctx", "tp"),
        check_vma=False,
    )
```
